512 devices in a mesh: src: 64 (over z, x_lo, core), tgt: 8 (over x_hi, y).
Axes of the slice: x: 4 (x_hi: 2, x_lo: 2; x = x_hi * 2 + x_lo), y: 4, z: 16, core: 2. Of those that a mesh axis runs over, the one named last changes fastest.
Arguments:
- source_cells: bfloat16 [1048576, 64], P('src'), may hold values from -6 to 6
- target_cells: bfloat16 [65536, 64], P(('tgt', 'src')), may hold values from -6 to 6
- start_potential: float32 [65536], P('tgt'), may hold values from -30 to 30
- source_logmass: float32 [1048576], P('src'), may hold values from -1 to 1
- target_logmass: float32 [65536], P('tgt'), may hold values from -1 to 1
- pair_src: int32 [64, 8, 256], P('src', 'tgt'), may hold values from 0 to 127, as said below
- pair_tgt: int32 [64, 8, 256], P('src', 'tgt'), may hold values from 0 to 63, as said below
- pair_count: int32 [64, 8], P('src', 'tgt'), may hold values from 64 to 256, as said below
Outputs:
- source_potential: float32 [1048576], P('src')
- target_potential: float32 [65536], P(('tgt', 'src'))
The draws below stay inside these ranges and needn't reach their ends.
Inputs may be any that keep to these rules, and one draw needn't show every extreme that they name: `pair_count`: on each device a whole number of slots is in use; in every draw some device uses all 256 slots. `pair_src`: no pair of blocks is listed twice on one device; every source block of a src index has a pair among the used slots of some device of that src index. `pair_tgt`: every target block of a tgt index has a pair among the used slots of some device of that tgt index.
All inputs are finite; a program needn't handle non-finite values.
Results may differ from the reference program's by a relative error of at most 0.0003.
Values may be sent and summed in bfloat16 or wider, within the bound.
No kernel may reach another device: no remote copies, remote signals or barrier semaphores. Data moves between devices by JAX's collectives and lax.ppermute only.
A program may use at most 64 MiB of HBM per device.

```python
import jax
import jax.numpy as jnp
from jax import lax

DIM = 64
BLK = 128
SB_DEV = 128
TB_DEV = 1
ITERS = 2
P_CAP = 256
TBT = 64
NS = 1048576
NT = 65536
N_SRC = 64
N_TGT = 8


def pair_tables(key):
    key_count, key_pick, key_perm, key_goal, key_first, key_second = jax.random.split(key, 6)
    counts = jax.random.randint(key_count, (N_SRC, N_TGT), P_CAP // 4, P_CAP + 1)
    chosen = jax.random.randint(key_pick, (), 0, N_SRC * N_TGT)
    flat_ids = jnp.arange(N_SRC * N_TGT).reshape(N_SRC, N_TGT)
    counts = jnp.where(flat_ids == chosen, P_CAP, counts)
    source_orders = jax.vmap(lambda sub_key: jax.random.permutation(sub_key, SB_DEV))(jax.random.split(key_perm, N_SRC))
    target_orders = jax.vmap(lambda sub_key: jax.random.permutation(sub_key, TBT))(jax.random.split(key_goal, N_TGT))
    slot_ids = jnp.arange(P_CAP)
    offsets = (slot_ids[None, None, :] % SB_DEV + SB_DEV // N_TGT * jnp.arange(N_TGT)[None, :, None]) % SB_DEV
    offsets = jnp.broadcast_to(offsets, (N_SRC, N_TGT, P_CAP))
    sources = jnp.take_along_axis(jnp.broadcast_to(source_orders[:, None, :], (N_SRC, N_TGT, SB_DEV)), offsets, axis=2)
    covering = jnp.minimum(TB_DEV * jnp.arange(N_SRC)[:, None, None] + jnp.arange(SB_DEV)[None, None, :], TBT - 1)
    covering = jnp.broadcast_to(covering, (N_SRC, N_TGT, SB_DEV))
    cover_blocks = jnp.take_along_axis(jnp.broadcast_to(target_orders[None, :, :], (N_SRC, N_TGT, TBT)), covering, axis=2)
    first_blocks = jax.random.randint(key_first, (N_SRC, N_TGT, SB_DEV), 0, TBT)
    first_blocks = jnp.where(jnp.arange(SB_DEV)[None, None, :] < TB_DEV, cover_blocks, first_blocks)
    second_blocks = (first_blocks + 1 + jax.random.randint(key_second, (N_SRC, N_TGT, SB_DEV), 0, TBT - 1)) % TBT
    targets = jnp.concatenate([first_blocks, second_blocks], axis=2)
    return (counts.astype(jnp.int32), sources.astype(jnp.int32), targets.astype(jnp.int32))


def draw_pair_count(key, part):
    return pair_tables(key)[0]


def draw_pair_src(key, part):
    return pair_tables(key)[1]


def draw_pair_tgt(key, part):
    return pair_tables(key)[2]


def draw_start_potential(key, part):
    key = jax.random.fold_in(key, 7)
    key_base = jax.random.fold_in(key, 0)
    values = jax.random.normal(key_base, (NT,), jnp.float32)
    return jnp.clip(values, -30.0, 30.0).astype(jnp.float32)


def shard_levels(rng, extent, pieces, least, high):
    gain = 1.0
    for position, blocks in pieces:
        draws = jax.random.uniform(jax.random.fold_in(jax.random.fold_in(rng, 6), position), (blocks,), jnp.float32, least / len(pieces), high / len(pieces))
        gain = gain * jnp.repeat(jnp.exp(draws), extent[position] // blocks).reshape((-1,) + (1,) * (len(extent) - 1 - position))
    return gain


def noise(key, shape, width, most, cuts=(), kind=jnp.bfloat16):
    array = jax.random.normal(key, shape, jnp.float32) * width
    if len(cuts) > 0:
        array = shard_levels(key, shape, cuts, -0.22, 0.18) * array
    return jnp.clip(array, min=-most, max=most).astype(kind)


def setup_inputs(seed: int = 0) -> dict:
    splits = jax.random.split(jax.random.key(seed), 9)
    source_cells = noise(splits[0], (NS, DIM), 1.0, 6.0, ((0, 64),))
    target_cells = noise(splits[1], (NT, DIM), 1.0, 6.0, ((0, 512),))
    start_potential = draw_start_potential(jax.random.fold_in(splits[8], 71), 0)
    source_logmass = jnp.clip(jax.random.uniform(splits[3], (NS,), jnp.float32, -1.0, 1.0) * shard_levels(splits[3], (NS,), ((0, 64),), -0.4, 0.0), -1.0, 1.0)
    target_logmass = jnp.clip(jax.random.uniform(splits[4], (NT,), jnp.float32, -1.0, 1.0) * shard_levels(splits[4], (NT,), ((0, 8),), -0.4, 0.0), -1.0, 1.0)
    pair_src = draw_pair_src(jax.random.fold_in(splits[8], 71), 0)
    pair_tgt = draw_pair_tgt(jax.random.fold_in(splits[8], 71), 0)
    pair_count = draw_pair_count(jax.random.fold_in(splits[8], 71), 0)
    return {"source_cells": source_cells, "target_cells": target_cells, "start_potential": start_potential, "source_logmass": source_logmass, "target_logmass": target_logmass, "pair_src": pair_src, "pair_tgt": pair_tgt, "pair_count": pair_count}


epsilon = 0.1
highest = lax.Precision.HIGHEST


def block_cost(source_blocks, target_blocks, src_rows, tgt_rows):
    src_cells = source_blocks[src_rows].astype(jnp.float32)
    tgt_cells = target_blocks[tgt_rows].astype(jnp.float32)
    products = jnp.einsum("pid,pjd->pij", src_cells, tgt_cells, precision=highest)
    src_norms = jnp.sum(src_cells * src_cells, axis=2)
    tgt_norms = jnp.sum(tgt_cells * tgt_cells, axis=2)
    return (src_norms[:, :, None] + tgt_norms[:, None, :] - 2.0 * products) / DIM


def combine_blocks(maxima, totals, owner_ids, in_use, owner_count):
    maxima = jnp.where(in_use[:, :, None], maxima, -jnp.inf).reshape(-1, BLK)
    totals = jnp.where(in_use[:, :, None], totals, 0.0).reshape(-1, BLK)
    owner_ids = owner_ids.reshape(-1)
    largest = jnp.full((owner_count, BLK), -jnp.inf, jnp.float32).at[owner_ids].max(maxima)
    summed = jnp.zeros((owner_count, BLK), jnp.float32).at[owner_ids].add(totals * jnp.exp(maxima - largest[owner_ids]))
    return largest + jnp.log(summed)


def reference(source_cells, target_cells, start_potential, source_logmass, target_logmass, pair_src, pair_tgt, pair_count):
    source_blocks = source_cells.reshape(-1, BLK, DIM)
    target_blocks = target_cells.reshape(-1, BLK, DIM)
    slot_ids = jnp.arange(P_CAP, dtype=jnp.int32)
    in_use = (slot_ids[None, None, :] < pair_count[:, :, None]).reshape(-1, P_CAP)
    src_global = (pair_src + (jnp.arange(N_SRC, dtype=jnp.int32) * SB_DEV)[:, None, None]).reshape(-1, P_CAP)
    tgt_global = (pair_tgt + (jnp.arange(N_TGT, dtype=jnp.int32) * TBT)[None, :, None]).reshape(-1, P_CAP)
    source_mass = source_logmass.reshape(-1, BLK)
    target_mass = target_logmass.reshape(-1, BLK)
    potential = start_potential
    source_potential = source_logmass
    for iteration in range(ITERS):
        target_values = potential.reshape(-1, BLK)

        def row_terms(pair_rows):
            src_rows, tgt_rows = pair_rows
            scores = (target_values[tgt_rows][:, None, :] - block_cost(source_blocks, target_blocks, src_rows, tgt_rows)) / epsilon
            row_max = jnp.max(scores, axis=2)
            return row_max, jnp.sum(jnp.exp(scores - row_max[:, :, None]), axis=2)

        maxima, totals = lax.map(row_terms, (src_global, tgt_global))
        source_values = epsilon * (source_mass - combine_blocks(maxima, totals, src_global, in_use, source_mass.shape[0]))

        def column_terms(pair_rows):
            src_rows, tgt_rows = pair_rows
            scores = (source_values[src_rows][:, :, None] - block_cost(source_blocks, target_blocks, src_rows, tgt_rows)) / epsilon
            column_max = jnp.max(scores, axis=1)
            return column_max, jnp.sum(jnp.exp(scores - column_max[:, None, :]), axis=1)

        maxima, totals = lax.map(column_terms, (src_global, tgt_global))
        potential = (epsilon * (target_mass - combine_blocks(maxima, totals, tgt_global, in_use, target_mass.shape[0]))).reshape(-1)
        source_potential = source_values.reshape(-1)
    return source_potential, potential
```

```python
import functools

import jax
import jax.numpy as jnp
from jax import lax
from jax.experimental import pallas as pl
from jax.experimental.pallas import tpu as pltpu
from jax.sharding import PartitionSpec as P

DIM = 64
BLK = 128
SLOTS = 256
EPS = 0.1
SCALE = 2.0 / (DIM * EPS)
LOG2E = 1.4426950408889634
KAPPA = SCALE * LOG2E
LOWEST = -1e30
UNROLL = 8
WAYS = 4
VMEM = pltpu.VMEM
SMEM = pltpu.SMEM
bf16 = jnp.bfloat16
f32 = jnp.float32


def nt_dot(a, b):
    return lax.dot_general(a, b, (((1,), (1,)), ((), ())), preferred_element_type=f32)


def split3(x):
    hi = x.astype(bf16).astype(f32)
    rest = x - hi
    mid = rest.astype(bf16).astype(f32)
    return hi, mid, rest - mid


def spread(potential, e1_ref, e2_ref):
    beta = potential * (1.0 / SCALE)
    for g in range(potential.shape[0] // 64):
        hi, mid, lo = split3(beta[g * 64 : g * 64 + 64])
        first = jnp.concatenate([jnp.zeros_like(hi), hi], axis=0)
        second = jnp.concatenate([mid, lo], axis=0)
        e1_ref[g] = first.T.astype(bf16)
        e2_ref[g] = second.T.astype(bf16)


def norm_row(block):
    x = block.astype(f32)
    square = x * x
    hi = square.astype(bf16)
    lo = (square - hi.astype(f32)).astype(bf16)
    ones = jnp.ones((16, BLK), bf16)
    return (nt_dot(ones, hi) + nt_dot(ones, lo))[:1]


def tall(row16):
    return jnp.concatenate([row16] * (BLK // 16), axis=0)


def pair_tile(x_ref, x_place, x_id, o_ref, o_place, e1_ref, e2_ref, hot_ref):
    g, r = x_id // 64, lax.rem(x_id, 64)
    left = jnp.concatenate([x_ref[x_place] + e1_ref[g], e2_ref[g]], axis=1)
    right = jnp.concatenate([o_ref[o_place] + tall(hot_ref[0, r]), tall(hot_ref[1, r])], axis=1)
    return nt_dot(left, right)


def over_pairs(count, pick, work):
    def group(n, carry):
        work([pick(n * UNROLL + q, n * UNROLL + q < count) for q in range(UNROLL)])
        return carry

    lax.fori_loop(0, (count + UNROLL - 1) // UNROLL, group, 0)


def fold_rows(accs, owners, combine):
    parts = []
    for g in range(owners // 8):
        total = None
        for acc in accs:
            for s in range(8):
                rows = acc[pl.ds(g * 64 + s, 8, stride=8), :]
                total = rows if total is None else combine(total, rows)
        parts.append(total)
    return jnp.concatenate(parts, axis=0)


def max_pass(count, pick, tile, accs, owners):
    for acc in accs:
        acc[...] = jnp.full(acc.shape, LOWEST, f32)

    def work(slots):
        tops = [jnp.max(tile(s).reshape(16, 8, BLK), axis=0) for s in slots]
        for q, (s, top) in enumerate(zip(slots, tops)):
            rows = pl.ds(pl.multiple_of(s["owner"] * 8, 8), 8)
            accs[q % WAYS][rows, :] = jnp.maximum(accs[q % WAYS][rows, :], top)

    over_pairs(count, pick, work)
    return fold_rows(accs, owners, jnp.maximum)


def sum_pass(count, pick, tile, accs, owners, offset_ref):
    for acc in accs:
        acc[...] = jnp.zeros(acc.shape, f32)

    def work(slots):
        sums = []
        for s in slots:
            offset = offset_ref[pl.ds(s["owner"], 1), :]
            sums.append(jnp.sum(jnp.exp2(tile(s) * KAPPA + offset).reshape(16, 8, BLK), axis=0))
        for q, (s, total) in enumerate(zip(slots, sums)):
            rows = pl.ds(pl.multiple_of(s["owner"] * 8, 8), 8)
            accs[q % WAYS][rows, :] = accs[q % WAYS][rows, :] + total

    over_pairs(count, pick, work)
    return fold_rows(accs, owners, jnp.add)


def picker(src_ref, tgt_ref, mine, by_source):
    def pick(k, used):
        s, t = src_ref[k], tgt_ref[k]
        s, t = jnp.where(used, s, 0), jnp.where(used, t, 0)
        place = lax.rem(t ^ mine, 4) * 16 + t // 4
        if by_source:
            return dict(x=t, x_place=place, o_place=s, owner=jnp.where(used, s, 128))
        return dict(x=s, x_place=s, o_place=place, owner=jnp.where(used, t, 64))

    return pick


def tiler(x_ref, o_ref, e1_ref, e2_ref, hot_ref):
    return lambda s: pair_tile(x_ref, s["x_place"], s["x"], o_ref, s["o_place"], e1_ref, e2_ref, hot_ref)


def stable_lse(count, pick, tile, accs, owners, offset_ref):
    top = max_pass(count, pick, tile, accs, owners)
    offset_ref[pl.ds(0, owners), :] = top * (-KAPPA)
    offset_ref[pl.ds(owners, 8), :] = jnp.zeros((8, BLK), f32)
    total = sum_pass(count, pick, tile, accs, owners, offset_ref)
    return jnp.where(total > 0.0, top * SCALE + jnp.log(jnp.maximum(total, 1e-37)), LOWEST)


def merge_lse(parts_ref):
    top = jnp.max(parts_ref[...], axis=0)
    total = jnp.sum(jnp.exp(parts_ref[...] - top[None]), axis=0)
    return top + jnp.log(total)


def first_kernel(info, src, tgt, cells, own, core, other, both, start, hot, out, packed, norms, e1, e2, offset, *accs):
    count, mine = info[0], info[1]
    lane = lax.broadcasted_iota(jnp.int32, (BLK // 2, BLK), 1)
    for d, part in enumerate((own, core, other, both)):

        def unpack(z, carry, d=d, part=part):
            half = part[z].astype(f32)
            low = jnp.where(lane < DIM, half, 0.0).astype(bf16)
            high = jnp.where(lane < DIM, pltpu.roll(half, DIM, 1), 0.0).astype(bf16)
            block = jnp.concatenate([low, high], axis=0)
            packed[d * 16 + z] = block
            norms[pl.ds(z * 4 + (d ^ mine), 1), :] = norm_row(block)
            return carry

        lax.fori_loop(0, 16, unpack, 0)
    spread(start[...] * (1.0 / EPS) - norms[...] * (SCALE / 2), e1, e2)
    tile = tiler(packed, cells, e1, e2, hot)
    lse = stable_lse(count, picker(src, tgt, mine, True), tile, accs, 128, offset)
    for k in range(8):
        out[k] = lse


def second_kernel(info, src, tgt, cells, packed, parts, mass, hot, out, potential, e1, e2, offset, *accs):
    count, mine = info[0], info[1]
    new = mass[...] - merge_lse(parts)
    potential[...] = new
    spread(new, e1, e2)
    tile = tiler(cells, packed, e1, e2, hot)
    lse = stable_lse(count, picker(src, tgt, mine, False), tile, accs, 64, offset)
    for k in range(4):
        out[k] = lse


def group_kernel(info, parts, out):
    lse = merge_lse(parts)
    half = jnp.where(info[2] == 0, lse[:32], lse[32:])
    for k in range(16):
        out[k] = half


def ring_kernel(parts, out):
    out[...] = merge_lse(parts)


def third_kernel(info, src, tgt, cells, packed, lse, mass, reference, hot, out, potential, e1, e2, offset, *accs):
    count, mine = info[0], info[1]
    new = mass[...] - lse[...]
    potential[...] = new
    spread(new, e1, e2)
    offset[pl.ds(0, 128), :] = reference[...] * LOG2E
    offset[pl.ds(128, 8), :] = jnp.zeros((8, BLK), f32)
    tile = tiler(packed, cells, e1, e2, hot)
    total = sum_pass(count, picker(src, tgt, mine, True), tile, accs, 128, offset)
    for k in range(8):
        out[k] = total


def fourth_kernel(info, src, tgt, cells, packed, parts, mass, former, reference, hot, out, final, e1, e2, offset, total, *accs):
    count, mine = info[0], info[1]
    new = former[...] + mass[...] - jnp.log(jnp.sum(parts[...], axis=0))
    spread(new, e1, e2)

    def finish(b, carry):
        final[pl.ds(b, 1), :] = norm_row(cells[b])
        return carry

    lax.fori_loop(0, 128, finish, 0)
    final[...] = EPS * (new + final[...] * (SCALE / 2))
    offset[pl.ds(0, 64), :] = reference[...] * LOG2E
    offset[pl.ds(64, 8), :] = jnp.zeros((8, BLK), f32)
    tile = tiler(cells, packed, e1, e2, hot)
    total[...] = sum_pass(count, picker(src, tgt, mine, False), tile, accs, 64, offset)
    for k in range(4):
        out[k] = total[pl.ds(k, 16, stride=4), :]


def total_kernel(parts, out):
    out[...] = jnp.sum(parts[...], axis=0)[:, None, :]


def last_kernel(info, parts, mass, potential, cells, out):
    me = info[3]
    total = jnp.sum(parts[...], axis=0)
    x = cells[...].astype(f32)
    square = x * x
    hi = square.astype(bf16)
    lo = (square - hi.astype(f32)).astype(bf16)
    ones = jnp.ones((16, DIM), bf16)
    norm = (nt_dot(ones, hi) + nt_dot(ones, lo))[:1]
    new = potential[pl.ds(me, 1), :] + mass[pl.ds(me, 1), :] - jnp.log(total)
    out[...] = EPS * (new + norm * (SCALE / 2))


def call(kernel, kinds, outs, scratch=()):
    specs = [pl.BlockSpec(memory_space=SMEM if kind == "s" else VMEM) for kind in kinds]
    out_specs = [pl.BlockSpec(memory_space=VMEM) for _ in outs]
    shapes = [jax.ShapeDtypeStruct(shape, dtype) for shape, dtype in outs]
    single = len(outs) == 1
    return pl.pallas_call(
        kernel,
        in_specs=specs,
        out_specs=out_specs[0] if single else out_specs,
        out_shape=shapes[0] if single else shapes,
        scratch_shapes=list(scratch),
        compiler_params=pltpu.CompilerParams(vmem_limit_bytes=40 * 1024 * 1024),
    )


def sweep_scratch(groups, owners):
    return [
        VMEM((groups, BLK, BLK), bf16),
        VMEM((groups, BLK, BLK), bf16),
        VMEM((owners + 8, BLK), f32),
    ]


def accumulators(owners):
    return [VMEM(((owners + 1) * 8, BLK), f32) for _ in range(WAYS)]


def on_device(source_cells, target_cells, start, source_logmass, target_logmass, pair_src, pair_tgt, pair_count):
    ring = [[z * 4 + r for z in range(16)] for r in range(4)]
    chips = [[z * 4 + r for r in range(4)] for z in range(16)]
    cores = [[i, i + 1] for i in range(0, 64, 2)]
    to_core = [(i, i ^ 1) for i in range(64)]
    to_chip = [(i, i ^ 2) for i in range(64)]

    me = lax.axis_index("src")
    mine = lax.rem(me, 4)
    info = jnp.stack([pair_count.reshape(()), mine, lax.rem(me, 2), me]).astype(jnp.int32)
    src, tgt = pair_src.reshape(-1), pair_tgt.reshape(-1)

    small = jnp.concatenate([target_cells[:64], target_cells[64:]], axis=1)
    own = lax.all_to_all(jnp.broadcast_to(small[None], (16, 64, BLK)), "src", 0, 0, axis_index_groups=ring)
    other = lax.ppermute(own, "src", to_chip)
    core = lax.ppermute(own, "src", to_core)
    both = lax.ppermute(other, "src", to_core)

    cells = jnp.pad(source_cells, ((0, 0), (0, BLK - DIM))).reshape(-1, BLK, BLK)
    source_mass = source_logmass.reshape(-1, BLK)
    target_mass = target_logmass.reshape(-1, BLK)
    first = jnp.arange(64)[:, None] + 64 == jnp.arange(BLK)[None, :]
    second = jnp.arange(64)[:, None] == jnp.arange(BLK)[None, :] % 64
    hot = jnp.broadcast_to(jnp.stack([first, second])[:, :, None, :], (2, 64, 16, BLK)).astype(bf16)

    parts, packed = call(
        first_kernel,
        "sssvvvvvvv",
        [((8, 128, BLK), f32), ((64, BLK, BLK), bf16)],
        [VMEM((64, BLK), f32)] + sweep_scratch(1, 128) + accumulators(128),
    )(info, src, tgt, cells, own, core, other, both, start.reshape(-1, BLK), hot)
    parts = lax.all_to_all(parts, "tgt", 0, 0)
    lse, first_u = call(
        second_kernel,
        "sssvvvvv",
        [((4, 64, BLK), f32), ((128, BLK), f32)],
        sweep_scratch(2, 64) + accumulators(64),
    )(info, src, tgt, cells, packed, parts, source_mass, hot)
    lse = lax.all_to_all(lse, "src", 0, 0, axis_index_groups=chips)
    lse = call(group_kernel, "sv", [((16, 32, BLK), f32)])(info, lse)
    lse = lax.all_to_all(lse, "src", 0, 0, axis_index_groups=ring)
    lse = call(ring_kernel, "v", [((32, BLK), f32)])(lse)
    lse = lax.all_gather(lse, "src", axis=0, axis_index_groups=cores, tiled=True)
    parts, first_v = call(
        third_kernel,
        "sssvvvvvv",
        [((8, 128, BLK), f32), ((64, BLK), f32)],
        sweep_scratch(1, 128) + accumulators(128),
    )(info, src, tgt, cells, packed, lse, target_mass, first_u, hot)
    parts = lax.all_to_all(parts, "tgt", 0, 0)
    sums, last_u = call(
        fourth_kernel,
        "sssvvvvvvv",
        [((4, 16, BLK), f32), ((128, BLK), f32)],
        sweep_scratch(2, 64) + [VMEM((64, BLK), f32)] + accumulators(64),
    )(info, src, tgt, cells, packed, parts, source_mass, first_u, first_v, hot)
    sums = lax.all_to_all(sums, "src", 0, 0, axis_index_groups=chips)
    sums = call(total_kernel, "v", [((16, 1, BLK), f32)])(sums)
    sums = lax.all_to_all(sums, "src", 0, 0, axis_index_groups=ring)
    last_v = call(last_kernel, "svvvv", [((1, BLK), f32)])(info, sums, target_mass, first_v, target_cells)
    return last_u.reshape(-1), last_v.reshape(-1)


def solution(mesh):
    in_specs = (
        P("src", None),
        P(("tgt", "src"), None),
        P("tgt"),
        P("src"),
        P("tgt"),
        P("src", "tgt", None),
        P("src", "tgt", None),
        P("src", "tgt"),
    )
    out_specs = (P("src"), P(("tgt", "src")))
    return jax.shard_map(
        on_device, mesh=mesh, in_specs=in_specs, out_specs=out_specs, check_vma=False
    )
```

```python
import functools

import jax
import jax.numpy as jnp
from jax import lax
from jax.experimental import pallas as pl
from jax.experimental.pallas import tpu as pltpu
from jax.sharding import PartitionSpec as P

DIM = 64
BLK = 128
EPS = 0.1
SCALE = 2.0 / (DIM * EPS)
LOG2E = 1.4426950408889634
KAPPA = SCALE * LOG2E
LOWEST = -1e30
UNROLL = 32
WAYS = 4
VMEM = pltpu.VMEM
SMEM = pltpu.SMEM
bf16 = jnp.bfloat16
f32 = jnp.float32


def block_of(n):
    return pl.ds(pl.multiple_of(n * BLK, BLK), BLK)


def as_rows(block):
    return jnp.concatenate([block, jnp.zeros((BLK - DIM, BLK), bf16)], axis=0).T


def norm_row(block):
    x = block.astype(f32)
    return jnp.sum(x * x, axis=0, keepdims=True)


def spread(potential, columns_ref, extra_ref):
    blocks = potential.shape[0]
    beta = potential * (1.0 / SCALE)
    hi = beta.astype(bf16).astype(f32)
    rest = beta - hi
    mid = rest.astype(bf16).astype(f32)
    for s, part in enumerate((hi, mid, rest - mid, jnp.zeros_like(hi))):
        columns_ref[pl.ds(s, blocks, stride=4), :] = part
    for g in range(blocks // 16):
        half = columns_ref[g * 64 : g * 64 + 64, :]
        extra_ref[g] = jnp.concatenate([jnp.zeros_like(half), half], axis=0).T.astype(bf16)


def pair_tile(x_ref, extra_ref, hot_ref, x_place, x_id, other_block):
    left = x_ref[x_place] + extra_ref[x_id // 16]
    right = jnp.concatenate([other_block, hot_ref[lax.rem(x_id, 16)]], axis=0)
    return jnp.dot(left, right, preferred_element_type=f32).reshape(16, 8, BLK)


def over_pairs(count, pick, work):
    def group(n, carry):
        work([pick(n * UNROLL + q, n * UNROLL + q < count) for q in range(UNROLL)])
        return carry

    lax.fori_loop(0, (count + UNROLL - 1) // UNROLL, group, 0)


def owner_rows(slot):
    return pl.ds(pl.multiple_of(slot["owner"] * 8, 8), 8)


def strided(accs, g):
    return [acc[pl.ds(g * 64 + s, 8, stride=8), :] for acc in accs for s in range(8)]


def stable_lse(count, pick, tile, tops, sums, owners):
    for top, total in zip(tops, sums):
        top[...] = jnp.full(top.shape, LOWEST, f32)
        total[...] = jnp.zeros(total.shape, f32)

    def work(slots):
        stats = []
        for s in slots:
            z = tile(s)
            most = jnp.max(z, axis=0)
            stats.append((most, jnp.sum(jnp.exp2((z - most[None]) * KAPPA), axis=0)))
        for q, (s, (most, part)) in enumerate(zip(slots, stats)):
            rows, top, total = owner_rows(s), tops[q % WAYS], sums[q % WAYS]
            old = top[rows, :]
            new = jnp.maximum(old, most)
            total[rows, :] = total[rows, :] * jnp.exp2((old - new) * KAPPA) + part * jnp.exp2((most - new) * KAPPA)
            top[rows, :] = new

    over_pairs(count, pick, work)
    out = []
    for g in range(owners // 8):
        rows = strided(tops, g)
        most = functools.reduce(jnp.maximum, rows)
        parts = [p * jnp.exp2((r - most) * KAPPA) for r, p in zip(rows, strided(sums, g))]
        total = functools.reduce(jnp.add, parts)
        out.append(jnp.where(total > 0.0, most * SCALE + jnp.log(jnp.maximum(total, 1e-30)), LOWEST))
    return jnp.concatenate(out, axis=0)


def plain_sum(count, pick, tile, sums, owners, offset_ref):
    for total in sums:
        total[...] = jnp.zeros(total.shape, f32)

    def work(slots):
        parts = []
        for s in slots:
            offset = offset_ref[pl.ds(s["owner"], 1), :]
            parts.append(jnp.sum(jnp.exp2(tile(s) * KAPPA + offset[None]), axis=0))
        for q, (s, part) in enumerate(zip(slots, parts)):
            rows, total = owner_rows(s), sums[q % WAYS]
            total[rows, :] = total[rows, :] + part

    over_pairs(count, pick, work)
    return jnp.concatenate([functools.reduce(jnp.add, strided(sums, g)) for g in range(owners // 8)], axis=0)


def place_of(t, mine):
    return lax.rem(t ^ mine, 4) * 16 + t // 4


def picker(src_ref, tgt_ref, by_source):
    def pick(k, used):
        s, t = jnp.where(used, src_ref[k], 0), jnp.where(used, tgt_ref[k], 0)
        return dict(s=s, t=t, owner=jnp.where(used, s, 128) if by_source else jnp.where(used, t, 64))

    return pick


def by_source(targets, sources, extra, hot, mine):
    return lambda p: pair_tile(targets, extra, hot, place_of(p["t"], mine), p["t"], sources[:, block_of(p["s"])])


def by_target(sources, targets, extra, hot, mine):
    return lambda p: pair_tile(sources, extra, hot, p["s"], p["s"], targets[place_of(p["t"], mine)])


def prepare_kernel(cells, rows, norms, hot):
    def some(n, carry):
        for q in range(16):
            block = cells[:, block_of(n * 16 + q)]
            rows[n * 16 + q] = as_rows(block)
            norms[pl.ds(n * 16 + q, 1), :] = norm_row(block)
        return carry

    lax.fori_loop(0, 8, some, 0)
    line = lax.broadcasted_iota(jnp.int32, (DIM, BLK), 0)
    for r in range(16):
        hot[r] = jnp.where((line >= 4 * r) & (line < 4 * r + 3), 1.0, 0.0).astype(bf16)


def merge_lse(parts_ref):
    top = jnp.max(parts_ref[...], axis=0)
    total = jnp.sum(jnp.exp(parts_ref[...] - top[None]), axis=0)
    return top + jnp.log(total)


def first_kernel(
    info, src, tgt, sources, own, core, other, both, start, hot, out, rows, targets, norms, columns, extra, *accs
):
    count, mine = info[0], info[1]
    for d, part in enumerate((own, core, other, both)):
        for z in range(16):
            block = part[z]
            targets[d * 16 + z] = block
            rows[d * 16 + z] = as_rows(block)
            norms[pl.ds(z * 4 + (d ^ mine), 1), :] = norm_row(block)
    spread(start[...] * (1.0 / EPS) - norms[...] * (SCALE / 2), columns, extra)
    tile = by_source(rows, sources, extra, hot, mine)
    lse = stable_lse(count, picker(src, tgt, True), tile, accs[:WAYS], accs[WAYS:], 128)
    for k in range(8):
        out[k] = lse


def second_kernel(info, src, tgt, rows, targets, parts, mass, hot, out, potential, columns, extra, *accs):
    count, mine = info[0], info[1]
    new = mass[...] - merge_lse(parts)
    potential[...] = new
    spread(new, columns, extra)
    tile = by_target(rows, targets, extra, hot, mine)
    lse = stable_lse(count, picker(src, tgt, False), tile, accs[:WAYS], accs[WAYS:], 64)
    for k in range(4):
        out[k] = lse


def group_kernel(info, parts, out):
    lse = merge_lse(parts)
    half = jnp.where(info[2] == 0, lse[:32], lse[32:])
    for k in range(16):
        out[k] = half


def ring_kernel(parts, out):
    out[...] = merge_lse(parts)


def third_kernel(
    info, src, tgt, sources, rows, lse, mass, reference, hot, out, potential, columns, extra, offset, *accs
):
    count, mine = info[0], info[1]
    new = mass[...] - lse[...]
    potential[...] = new
    spread(new, columns, extra)
    offset[pl.ds(0, 128), :] = reference[...] * LOG2E
    offset[pl.ds(128, 8), :] = jnp.zeros((8, BLK), f32)
    tile = by_source(rows, sources, extra, hot, mine)
    total = plain_sum(count, picker(src, tgt, True), tile, accs, 128, offset)
    for k in range(8):
        out[k] = total


def fourth_kernel(
    info, src, tgt, rows, targets, parts, mass, former, reference, norms, hot,
    out, final, columns, extra, offset, total, *accs,
):
    count, mine = info[0], info[1]
    new = former[...] + mass[...] - jnp.log(jnp.sum(parts[...], axis=0))
    spread(new, columns, extra)
    final[...] = EPS * (new + norms[...] * (SCALE / 2))
    offset[pl.ds(0, 64), :] = reference[...] * LOG2E
    offset[pl.ds(64, 8), :] = jnp.zeros((8, BLK), f32)
    tile = by_target(rows, targets, extra, hot, mine)
    total[...] = plain_sum(count, picker(src, tgt, False), tile, accs, 64, offset)
    for k in range(4):
        out[k] = total[pl.ds(k, 16, stride=4), :]


def total_kernel(parts, out):
    out[...] = jnp.sum(parts[...], axis=0)[:, None, :]


def last_kernel(info, parts, mass, potential, cells, out):
    me = info[3]
    total = jnp.sum(parts[...], axis=0)
    new = potential[pl.ds(me, 1), :] + mass[pl.ds(me, 1), :] - jnp.log(total)
    out[...] = EPS * (new + norm_row(cells[...]) * (SCALE / 2))


def call(kernel, kinds, outs, scratch=()):
    specs = [pl.BlockSpec(memory_space=SMEM if kind == "s" else VMEM) for kind in kinds]
    out_specs = [pl.BlockSpec(memory_space=VMEM) for _ in outs]
    shapes = [jax.ShapeDtypeStruct(shape, dtype) for shape, dtype in outs]
    single = len(outs) == 1
    return pl.pallas_call(
        kernel,
        in_specs=specs,
        out_specs=out_specs[0] if single else out_specs,
        out_shape=shapes[0] if single else shapes,
        scratch_shapes=list(scratch),
        compiler_params=pltpu.CompilerParams(vmem_limit_bytes=32 * 1024 * 1024),
        name=kernel.__name__,
    )


def columns_of(blocks):
    return [VMEM((blocks * 4, BLK), f32), VMEM((blocks // 16, BLK, BLK), bf16)]


def accumulators(owners, kinds):
    return [VMEM(((owners + 1) * 8, BLK), f32) for _ in range(WAYS * kinds)]


def on_device(source_cells, target_cells, start, source_logmass, target_logmass, pair_src, pair_tgt, pair_count):
    ring = [[z * 4 + r for z in range(16)] for r in range(4)]
    chips = [[z * 4 + r for r in range(4)] for z in range(16)]
    cores = [[i, i + 1] for i in range(0, 64, 2)]
    to_core = [(i, i ^ 1) for i in range(64)]
    to_chip = [(i, i ^ 2) for i in range(64)]

    me = lax.axis_index("src")
    info = jnp.stack([pair_count.reshape(()), lax.rem(me, 4), lax.rem(me, 2), me]).astype(jnp.int32)
    src, tgt = pair_src.reshape(-1), pair_tgt.reshape(-1)

    mine = target_cells.T
    own = lax.all_to_all(jnp.broadcast_to(mine[None], (16, DIM, BLK)), "src", 0, 0, axis_index_groups=ring)
    other = lax.ppermute(own, "src", to_chip)
    core = lax.ppermute(own, "src", to_core)
    both = lax.ppermute(other, "src", to_core)

    sources = source_cells.T
    source_mass = source_logmass.reshape(-1, BLK)
    target_mass = target_logmass.reshape(-1, BLK)
    rows, norms, hot = call(
        prepare_kernel, "v", [((128, BLK, BLK), bf16), ((128, BLK), f32), ((16, DIM, BLK), bf16)]
    )(sources)

    parts, target_rows, targets = call(
        first_kernel,
        "sssvvvvvvv",
        [((8, 128, BLK), f32), ((64, BLK, BLK), bf16), ((64, DIM, BLK), bf16)],
        [VMEM((64, BLK), f32)] + columns_of(64) + accumulators(128, 2),
    )(info, src, tgt, sources, own, core, other, both, start.reshape(-1, BLK), hot)
    parts = lax.all_to_all(parts, "tgt", 0, 0)
    lse, first_u = call(
        second_kernel,
        "sssvvvvv",
        [((4, 64, BLK), f32), ((128, BLK), f32)],
        columns_of(128) + accumulators(64, 2),
    )(info, src, tgt, rows, targets, parts, source_mass, hot)
    lse = lax.all_to_all(lse, "src", 0, 0, axis_index_groups=chips)
    lse = call(group_kernel, "sv", [((16, 32, BLK), f32)])(info, lse)
    lse = lax.all_to_all(lse, "src", 0, 0, axis_index_groups=ring)
    lse = call(ring_kernel, "v", [((32, BLK), f32)])(lse)
    lse = lax.all_gather(lse, "src", axis=0, axis_index_groups=cores, tiled=True)
    parts, first_v = call(
        third_kernel,
        "sssvvvvvv",
        [((8, 128, BLK), f32), ((64, BLK), f32)],
        columns_of(64) + [VMEM((136, BLK), f32)] + accumulators(128, 1),
    )(info, src, tgt, sources, target_rows, lse, target_mass, first_u, hot)
    parts = lax.all_to_all(parts, "tgt", 0, 0)
    sums, last_u = call(
        fourth_kernel,
        "sssvvvvvvvv",
        [((4, 16, BLK), f32), ((128, BLK), f32)],
        columns_of(128) + [VMEM((72, BLK), f32), VMEM((64, BLK), f32)] + accumulators(64, 1),
    )(info, src, tgt, rows, targets, parts, source_mass, first_u, first_v, norms, hot)
    sums = lax.all_to_all(sums, "src", 0, 0, axis_index_groups=chips)
    sums = call(total_kernel, "v", [((16, 1, BLK), f32)])(sums)
    sums = lax.all_to_all(sums, "src", 0, 0, axis_index_groups=ring)
    last_v = call(last_kernel, "svvvv", [((1, BLK), f32)])(info, sums, target_mass, first_v, mine)
    return last_u.reshape(-1), last_v.reshape(-1)


def solution(mesh):
    in_specs = (
        P("src", None),
        P(("tgt", "src"), None),
        P("tgt"),
        P("src"),
        P("tgt"),
        P("src", "tgt", None),
        P("src", "tgt", None),
        P("src", "tgt"),
    )
    out_specs = (P("src"), P(("tgt", "src")))
    return jax.shard_map(
        on_device, mesh=mesh, in_specs=in_specs, out_specs=out_specs, check_vma=False
    )
```

```python
import functools

import jax
import jax.numpy as jnp
from jax import lax
from jax.experimental import pallas as pl
from jax.experimental.pallas import tpu as pltpu
from jax.sharding import PartitionSpec as P

DIM = 64
BLK = 128
EPS = 0.1
SCALE = 2.0 / (DIM * EPS)
LOG2E = 1.4426950408889634
KAPPA = SCALE * LOG2E
LOWEST = -1e30
CHUNKS = 8
UNROLL = 64
WAYS = 4
VMEM = pltpu.VMEM
SMEM = pltpu.SMEM
bf16 = jnp.bfloat16
f32 = jnp.float32


def block_of(n):
    return pl.ds(pl.multiple_of(n * BLK, BLK), BLK)


def as_rows(block):
    return jnp.concatenate([block, jnp.zeros((BLK - DIM, BLK), bf16)], axis=0).T


def norm_row(block):
    x = block.astype(f32)
    return jnp.sum(x * x, axis=0, keepdims=True)


def spread(potential, columns_ref, extra_ref):
    blocks = potential.shape[0]
    beta = potential * (1.0 / SCALE)
    hi = beta.astype(bf16).astype(f32)
    rest = beta - hi
    mid = rest.astype(bf16).astype(f32)
    for s, part in enumerate((hi, mid, rest - mid, jnp.zeros_like(hi))):
        columns_ref[pl.ds(s, blocks, stride=4), :] = part
    for g in range(blocks // 16):
        half = columns_ref[g * 64 : g * 64 + 64, :]
        extra_ref[g] = jnp.concatenate([jnp.zeros_like(half), half], axis=0).T.astype(bf16)


def pair_tile(x_ref, extra_ref, hot_ref, x_place, x_id, other_block):
    left = x_ref[x_place] + extra_ref[x_id // 16]
    right = jnp.concatenate([other_block, hot_ref[lax.rem(x_id, 16)]], axis=0)
    return jnp.dot(left, right, preferred_element_type=f32).reshape(16, 8, BLK)


def over_pairs(count, pick, work):
    def group(n, carry):
        work([pick(n * UNROLL + q, n * UNROLL + q < count) for q in range(UNROLL)])
        return carry

    lax.fori_loop(0, (count + UNROLL - 1) // UNROLL, group, 0)


def owner_rows(slot):
    return pl.ds(pl.multiple_of(slot["owner"] * 8, 8), 8)


def strided(accs, g):
    return [acc[pl.ds(g * 64 + s, 8, stride=8), :] for acc in accs for s in range(8)]


def stable_lse(count, pick, tile, tops, sums, owners):
    for top, total in zip(tops, sums):
        top[...] = jnp.full(top.shape, LOWEST, f32)
        total[...] = jnp.zeros(total.shape, f32)

    def work(slots):
        stats = []
        for s in slots:
            z = tile(s)
            most = jnp.max(z, axis=0)
            stats.append((most, jnp.sum(jnp.exp2((z - most[None]) * KAPPA), axis=0)))
        for q, (s, (most, part)) in enumerate(zip(slots, stats)):
            rows, top, total = owner_rows(s), tops[q % WAYS], sums[q % WAYS]
            old = top[rows, :]
            new = jnp.maximum(old, most)
            total[rows, :] = total[rows, :] * jnp.exp2((old - new) * KAPPA) + part * jnp.exp2((most - new) * KAPPA)
            top[rows, :] = new

    over_pairs(count, pick, work)
    out = []
    for g in range(owners // 8):
        rows = strided(tops, g)
        most = functools.reduce(jnp.maximum, rows)
        parts = [p * jnp.exp2((r - most) * KAPPA) for r, p in zip(rows, strided(sums, g))]
        total = functools.reduce(jnp.add, parts)
        out.append(jnp.where(total > 0.0, most * SCALE + jnp.log(jnp.maximum(total, 1e-30)), LOWEST))
    return jnp.concatenate(out, axis=0)


def plain_sum(count, pick, tile, total, owners, offset_ref):
    total[...] = jnp.zeros(total.shape, f32)

    def work(slots):
        parts = []
        for s in slots:
            offset = offset_ref[pl.ds(s["owner"], 1), :]
            parts.append(jnp.sum(jnp.exp2(tile(s) * KAPPA + offset[None]), axis=0))
        for s, part in zip(slots, parts):
            rows = owner_rows(s)
            total[rows, :] = total[rows, :] + part

    over_pairs(count, pick, work)
    return jnp.concatenate([functools.reduce(jnp.add, strided([total], g)) for g in range(owners // 8)], axis=0)


def place_of(t, mine):
    return lax.rem(t ^ mine, 4) * 16 + t // 4


def picker(src_ref, tgt_ref, by_source):
    def pick(k, used):
        s, t = jnp.where(used, src_ref[k], 0), jnp.where(used, tgt_ref[k], 0)
        return dict(s=s, t=t, owner=jnp.where(used, s, 128) if by_source else jnp.where(used, t, 64))

    return pick


def by_source(targets, sources, extra, hot, mine):
    return lambda p: pair_tile(targets, extra, hot, place_of(p["t"], mine), p["t"], sources[:, block_of(p["s"])])


def by_target(sources, targets, extra, hot, mine):
    return lambda p: pair_tile(sources, extra, hot, p["s"], p["s"], targets[place_of(p["t"], mine)])


def prepare_kernel(cells, sources, rows, norms, hot, sems):
    width = sources.shape[1] // CHUNKS

    def chunk(n):
        part = pl.ds(n * width, width)
        return pltpu.make_async_copy(cells.at[:, part], sources.at[:, part], sems.at[n])

    for n in range(CHUNKS):
        chunk(n).start()
    line = lax.broadcasted_iota(jnp.int32, (DIM, BLK), 0)
    for r in range(16):
        hot[r] = jnp.where((line >= 4 * r) & (line < 4 * r + 3), 1.0, 0.0).astype(bf16)
    for n in range(CHUNKS):
        chunk(n).wait()
        for q in range(128 // CHUNKS):
            b = n * (128 // CHUNKS) + q
            block = sources[:, b * BLK : b * BLK + BLK]
            rows[b] = as_rows(block)
            norms[b : b + 1, :] = norm_row(block)


def merge_lse(parts_ref):
    top = jnp.max(parts_ref[...], axis=0)
    total = jnp.sum(jnp.exp(parts_ref[...] - top[None]), axis=0)
    return top + jnp.log(total)


def first_kernel(
    info, src, tgt, sources, own, core, other, both, start, hot, out, rows, targets, norms, columns, extra, *accs
):
    count, mine = info[0], info[1]
    for d, part in enumerate((own, core, other, both)):
        for z in range(16):
            block = part[z]
            targets[d * 16 + z] = block
            rows[d * 16 + z] = as_rows(block)
            norms[pl.ds(z * 4 + (d ^ mine), 1), :] = norm_row(block)
    spread(start[...] * (1.0 / EPS) - norms[...] * (SCALE / 2), columns, extra)
    tile = by_source(rows, sources, extra, hot, mine)
    lse = stable_lse(count, picker(src, tgt, True), tile, accs[:WAYS], accs[WAYS:], 128)
    for k in range(8):
        out[k] = lse


def second_kernel(info, src, tgt, rows, targets, parts, mass, hot, out, potential, columns, extra, *accs):
    count, mine = info[0], info[1]
    new = mass[...] - merge_lse(parts)
    potential[...] = new
    spread(new, columns, extra)
    tile = by_target(rows, targets, extra, hot, mine)
    lse = stable_lse(count, picker(src, tgt, False), tile, accs[:WAYS], accs[WAYS:], 64)
    for k in range(4):
        out[k] = lse[16 * k : 16 * k + 16]


def group_kernel(parts, out):
    lse = merge_lse(parts)
    for k in range(16):
        out[k] = lse


def ring_kernel(parts, out):
    out[...] = merge_lse(parts)


def third_kernel(
    info, src, tgt, sources, rows, lse, mass, reference, hot, out, potential, columns, extra, offset, acc
):
    count, mine = info[0], info[1]
    new = mass[...] - lse[...]
    potential[...] = new
    spread(new, columns, extra)
    offset[pl.ds(0, 128), :] = reference[...] * LOG2E
    offset[pl.ds(128, 8), :] = jnp.zeros((8, BLK), f32)
    tile = by_source(rows, sources, extra, hot, mine)
    total = plain_sum(count, picker(src, tgt, True), tile, acc, 128, offset)
    for k in range(8):
        out[k] = total


def fourth_kernel(
    info, src, tgt, rows, targets, parts, mass, former, reference, norms, hot,
    out, final, columns, extra, offset, acc,
):
    count, mine = info[0], info[1]
    new = former[...] + mass[...] - jnp.log(jnp.sum(parts[...], axis=0))
    spread(new, columns, extra)
    final[...] = EPS * (new + norms[...] * (SCALE / 2))
    offset[pl.ds(0, 64), :] = reference[...] * LOG2E
    offset[pl.ds(64, 8), :] = jnp.zeros((8, BLK), f32)
    tile = by_target(rows, targets, extra, hot, mine)
    out[...] = plain_sum(count, picker(src, tgt, False), tile, acc, 64, offset)


def total_kernel(info, parts, out):
    even, odd = [parts[0, pl.ds(k, 32, stride=2), :] + parts[1, pl.ds(k, 32, stride=2), :] for k in range(2)]
    out[...] = jnp.where(info[2] == 0, even, odd)[:, None, :]


def last_kernel(info, parts, mass, potential, cells, out):
    me = info[3]
    total = jnp.sum(parts[...], axis=0)
    new = potential[pl.ds(me, 1), :] + mass[pl.ds(me, 1), :] - jnp.log(total)
    out[...] = EPS * (new + norm_row(cells[...]) * (SCALE / 2))


def call(kernel, kinds, outs, scratch=()):
    spaces = {"s": SMEM, "v": VMEM, "a": pl.ANY}
    specs = [pl.BlockSpec(memory_space=spaces[kind]) for kind in kinds]
    out_specs = [pl.BlockSpec(memory_space=VMEM) for _ in outs]
    shapes = [jax.ShapeDtypeStruct(shape, dtype) for shape, dtype in outs]
    single = len(outs) == 1
    return pl.pallas_call(
        kernel,
        in_specs=specs,
        out_specs=out_specs[0] if single else out_specs,
        out_shape=shapes[0] if single else shapes,
        scratch_shapes=list(scratch),
        compiler_params=pltpu.CompilerParams(vmem_limit_bytes=32 * 1024 * 1024),
        name=kernel.__name__,
    )


def columns_of(blocks):
    return [VMEM((blocks * 4, BLK), f32), VMEM((blocks // 16, BLK, BLK), bf16)]


def accumulators(owners, number):
    return [VMEM(((owners + 1) * 8, BLK), f32) for _ in range(number)]


def on_device(source_cells, target_cells, start, source_logmass, target_logmass, pair_src, pair_tgt, pair_count):
    ring = [[z * 4 + r for z in range(16)] for r in range(4)]
    chips = [[z * 4 + r for r in range(4)] for z in range(16)]
    cores = [[i, i + 1] for i in range(0, 64, 2)]
    halves = [[2 * i + c for i in range(32)] for c in range(2)]
    to_core = [(i, i ^ 1) for i in range(64)]
    to_chip = [(i, i ^ 2) for i in range(64)]

    me = lax.axis_index("src")
    info = jnp.stack([pair_count.reshape(()), lax.rem(me, 4), lax.rem(me, 2), me]).astype(jnp.int32)
    src, tgt = pair_src.reshape(-1), pair_tgt.reshape(-1)
    source_mass = source_logmass.reshape(-1, BLK)
    target_mass = target_logmass.reshape(-1, BLK)

    mine = target_cells.T
    own = lax.all_to_all(jnp.broadcast_to(mine[None], (16, DIM, BLK)), "src", 0, 0, axis_index_groups=ring)
    other = lax.ppermute(own, "src", to_chip)
    core = lax.ppermute(own, "src", to_core)
    sources, rows, norms, hot = call(
        prepare_kernel,
        "a",
        [((DIM, 128 * BLK), bf16), ((128, BLK, BLK), bf16), ((128, BLK), f32), ((16, DIM, BLK), bf16)],
        [pltpu.SemaphoreType.DMA((CHUNKS,))],
    )(source_cells.T)
    other, hot = lax.optimization_barrier((other, hot))
    both = lax.ppermute(other, "src", to_core)

    parts, target_rows, targets = call(
        first_kernel,
        "sssvvvvvvv",
        [((8, 128, BLK), f32), ((64, BLK, BLK), bf16), ((64, DIM, BLK), bf16)],
        [VMEM((64, BLK), f32)] + columns_of(64) + accumulators(128, 2 * WAYS),
    )(info, src, tgt, sources, own, core, other, both, start.reshape(-1, BLK), hot)
    parts = lax.all_to_all(parts, "tgt", 0, 0)
    lse, first_u = call(
        second_kernel,
        "sssvvvvv",
        [((4, 16, BLK), f32), ((128, BLK), f32)],
        columns_of(128) + accumulators(64, 2 * WAYS),
    )(info, src, tgt, rows, targets, parts, source_mass, hot)
    lse = lax.all_to_all(lse, "src", 0, 0, axis_index_groups=chips)
    lse = call(group_kernel, "v", [((16, 16, BLK), f32)])(lse)
    lse = lax.all_to_all(lse, "src", 0, 0, axis_index_groups=ring)
    lse = call(ring_kernel, "v", [((16, BLK), f32)])(lse)
    lse = lax.all_gather(lse, "src", axis=0, axis_index_groups=chips, tiled=True)
    parts, first_v = call(
        third_kernel,
        "sssvvvvvv",
        [((8, 128, BLK), f32), ((64, BLK), f32)],
        columns_of(64) + [VMEM((136, BLK), f32)] + accumulators(128, 1),
    )(info, src, tgt, sources, target_rows, lse, target_mass, first_u, hot)
    parts = lax.all_to_all(parts, "tgt", 0, 0)
    sums, last_u = call(
        fourth_kernel,
        "sssvvvvvvvv",
        [((64, BLK), f32), ((128, BLK), f32)],
        columns_of(128) + [VMEM((72, BLK), f32)] + accumulators(64, 1),
    )(info, src, tgt, rows, targets, parts, source_mass, first_u, first_v, norms, hot)
    sums = lax.all_gather(sums, "src", axis=0, axis_index_groups=cores)
    sums = call(total_kernel, "sv", [((32, 1, BLK), f32)])(info, sums)
    sums = lax.all_to_all(sums, "src", 0, 0, axis_index_groups=halves)
    last_v = call(last_kernel, "svvvv", [((1, BLK), f32)])(info, sums, target_mass, first_v, mine)
    return last_u.reshape(-1), last_v.reshape(-1)


def solution(mesh):
    in_specs = (
        P("src", None),
        P(("tgt", "src"), None),
        P("tgt"),
        P("src"),
        P("tgt"),
        P("src", "tgt", None),
        P("src", "tgt", None),
        P("src", "tgt"),
    )
    out_specs = (P("src"), P(("tgt", "src")))
    return jax.shard_map(
        on_device, mesh=mesh, in_specs=in_specs, out_specs=out_specs, check_vma=False
    )
```

```python
import functools

import jax
import jax.numpy as jnp
from jax import lax
from jax.experimental import pallas as pl
from jax.experimental.pallas import tpu as pltpu
from jax.sharding import PartitionSpec as P

DIM = 64
BLK = 128
EPS = 0.1
SCALE = 2.0 / (DIM * EPS)
LOG2E = 1.4426950408889634
KAPPA = SCALE * LOG2E
LOWEST = -1e30
OWNER = 20
VMEM_LIMIT = 16 * 1024 * 1024
STEP_BITS = 6
UNROLL = 1 << STEP_BITS
WAYS = 4
VMEM = pltpu.VMEM
SMEM = pltpu.SMEM
bf16 = jnp.bfloat16
f32 = jnp.float32


def block_of(n):
    return pl.ds(pl.multiple_of(n * BLK, BLK), BLK)


def as_rows(block):
    return jnp.concatenate([block, jnp.zeros((BLK - DIM, BLK), bf16)], axis=0).T


def norm_row(block):
    x = block.astype(f32)
    return jnp.sum(x * x, axis=0, keepdims=True)


def spread(potential, columns_ref, extra_ref):
    blocks = potential.shape[0]
    beta = potential * (1.0 / SCALE)
    hi = beta.astype(bf16).astype(f32)
    rest = beta - hi
    mid = rest.astype(bf16).astype(f32)
    for s, part in enumerate((hi, mid, rest - mid, jnp.zeros_like(hi))):
        columns_ref[pl.ds(s, blocks, stride=4), :] = part
    for g in range(blocks // 16):
        half = columns_ref[g * 64 : g * 64 + 64, :]
        extra_ref[g] = jnp.concatenate([jnp.zeros_like(half), half], axis=0).T.astype(bf16)


def pair_tile(x_ref, extra_ref, hot_ref, x_place, x_id, other_block):
    left = x_ref[x_place] + extra_ref[x_id >> 4]
    right = jnp.concatenate([other_block, hot_ref[x_id & 15]], axis=0)
    return jnp.dot(left, right, preferred_element_type=f32).reshape(16, 8, BLK)


def over_pairs(info, work):
    def group(n, carry):
        row, first = 1 + (n >> (7 - STEP_BITS)), (n << STEP_BITS) & 127
        work([info[row, first + q] for q in range(UNROLL)])
        return carry

    lax.fori_loop(0, info[0, 1], group, 0)


def owner_rows(code):
    return pl.ds(pl.multiple_of(code >> OWNER, 8), 8)


def strided(accs, g):
    return [acc[pl.ds(g * 64 + s, 8, stride=8), :] for acc in accs for s in range(8)]


def stable_lse(info, tile, tops, sums, owners):
    for top, total in zip(tops, sums):
        top[...] = jnp.full(top.shape, LOWEST, f32)
        total[...] = jnp.zeros(total.shape, f32)

    def work(slots):
        stats = []
        for s in slots:
            z = tile(s)
            most = jnp.max(z, axis=0)
            stats.append((most, jnp.sum(jnp.exp2((z - most[None]) * KAPPA), axis=0)))
        for q, (s, (most, part)) in enumerate(zip(slots, stats)):
            rows, top, total = owner_rows(s), tops[q % WAYS], sums[q % WAYS]
            old = top[rows, :]
            new = jnp.maximum(old, most)
            total[rows, :] = total[rows, :] * jnp.exp2((old - new) * KAPPA) + part * jnp.exp2((most - new) * KAPPA)
            top[rows, :] = new

    over_pairs(info, work)
    out = []
    for g in range(owners // 8):
        rows = strided(tops, g)
        most = functools.reduce(jnp.maximum, rows)
        parts = [p * jnp.exp2((r - most) * KAPPA) for r, p in zip(rows, strided(sums, g))]
        total = functools.reduce(jnp.add, parts)
        out.append(jnp.where(total > 0.0, most * SCALE + jnp.log(jnp.maximum(total, 1e-30)), LOWEST))
    return jnp.concatenate(out, axis=0)


def plain_sum(info, tile, total, owners, offset):
    total[...] = jnp.zeros(total.shape, f32)

    def work(slots):
        parts = []
        for s in slots:
            parts.append(jnp.sum(jnp.exp2(tile(s) * KAPPA + offset[owner_rows(s), :][None]), axis=0))
        for s, part in zip(slots, parts):
            rows = owner_rows(s)
            total[rows, :] = total[rows, :] + part

    over_pairs(info, work)
    return jnp.concatenate([functools.reduce(jnp.add, strided([total], g)) for g in range(owners // 8)], axis=0)


def repeat_rows(values, offset):
    owners = values.shape[0]
    for k in range(8):
        offset[pl.ds(k, owners, stride=8), :] = values
    offset[pl.ds(owners * 8, 8), :] = jnp.zeros((8, BLK), f32)


def by_source(targets, sources, extra, hot):
    def tile(code):
        at = pl.multiple_of(code & 0x3F80, BLK)
        return pair_tile(targets, extra, hot, (code >> 14) & 63, code & 63, sources[:, pl.ds(at, BLK)])

    return tile


def by_target(sources, targets, extra, hot):
    def tile(code):
        s = code & 127
        return pair_tile(sources, extra, hot, s, s, targets[(code >> 14) & 63])

    return tile


def prepare_kernel(sources, pair_src, pair_tgt, pair_count, rows, norms, hot, by_src, by_tgt):
    me = lax.axis_index("src")
    lane = lax.broadcasted_iota(jnp.int32, (1, BLK), 1)
    count = jnp.broadcast_to(pair_count[...], (1, BLK))
    steps = (count + (UNROLL - 1)) >> STEP_BITS
    for k, value in enumerate((me, me & 1, me & 3, steps, count)):
        head = value if k == 0 else jnp.where(lane == 4 - k, value, head)
    by_src[0:1, :] = jnp.broadcast_to(head, (1, BLK))
    by_tgt[0:1, :] = jnp.broadcast_to(head, (1, BLK))
    for half in range(2):
        used = lane + half * BLK < count
        part = slice(half * BLK, (half + 1) * BLK)
        s, t = jnp.where(used, pair_src[:, part], 0), jnp.where(used, pair_tgt[:, part], 0)
        place = (((t ^ me) & 3) << 4) + (t >> 2)
        by_src[half + 1 : half + 2, :] = t + (s << 7) + (place << 14) + (jnp.where(used, s, 128) << (OWNER + 3))
        by_tgt[half + 1 : half + 2, :] = s + (place << 14) + (jnp.where(used, t, 64) << (OWNER + 3))
    line = lax.broadcasted_iota(jnp.int32, (DIM, BLK), 0)
    for r in range(16):
        hot[r] = jnp.where((line >= 4 * r) & (line < 4 * r + 3), 1.0, 0.0).astype(bf16)
    for b in range(128):
        block = sources[:, b * BLK : b * BLK + BLK]
        rows[b] = as_rows(block)
        norms[b : b + 1, :] = norm_row(block)


def merge_lse(parts_ref):
    top = jnp.max(parts_ref[...], axis=0)
    total = jnp.sum(jnp.exp(parts_ref[...] - top[None]), axis=0)
    return top + jnp.log(total)


def first_kernel(
    info, sources, own, core, other, both, start, hot, out, rows, targets, norms, columns, extra, *accs
):
    mine = info[0, 2]
    for d, part in enumerate((own, core, other, both)):
        for z in range(16):
            block = part[z]
            targets[d * 16 + z] = block
            rows[d * 16 + z] = as_rows(block)
            norms[pl.ds(z * 4 + (d ^ mine), 1), :] = norm_row(block)
    spread(start[...] * (1.0 / EPS) - norms[...] * (SCALE / 2), columns, extra)
    tile = by_source(rows, sources, extra, hot)
    lse = stable_lse(info, tile, accs[:WAYS], accs[WAYS:], 128)
    for k in range(8):
        out[k] = lse


def second_kernel(info, rows, targets, parts, mass, hot, out, potential, columns, extra, *accs):
    new = mass[...] - merge_lse(parts)
    potential[...] = new
    spread(new, columns, extra)
    tile = by_target(rows, targets, extra, hot)
    lse = stable_lse(info, tile, accs[:WAYS], accs[WAYS:], 64)
    for k in range(4):
        out[k] = lse[16 * k : 16 * k + 16]


def group_kernel(parts, out):
    lse = merge_lse(parts)
    for k in range(16):
        out[k] = lse


def ring_kernel(parts, out):
    out[...] = merge_lse(parts)


def third_kernel(
    info, sources, rows, lse, mass, reference, hot, mine, out, potential, base, columns, extra, offset, acc
):
    me = info[0, 4]
    new = mass[...] - lse[...]
    potential[...] = new
    base[...] = potential[pl.ds(me, 1), :] + mass[pl.ds(me, 1), :] + norm_row(mine[...]) * (SCALE / 2)
    spread(new, columns, extra)
    repeat_rows(reference[...] * LOG2E, offset)
    tile = by_source(rows, sources, extra, hot)
    total = plain_sum(info, tile, acc, 128, offset)
    for k in range(8):
        out[k] = total


def fourth_kernel(
    info, rows, targets, parts, mass, former, reference, norms, hot,
    out, final, odd, columns, extra, offset, acc,
):
    new = former[...] + mass[...] - jnp.log(jnp.sum(parts[...], axis=0))
    spread(new, columns, extra)
    final[...] = EPS * (new + norms[...] * (SCALE / 2))
    odd[...] = jnp.full(odd.shape, info[0, 3], jnp.int32)
    repeat_rows(reference[...] * LOG2E, offset)
    tile = by_target(rows, targets, extra, hot)
    out[...] = plain_sum(info, tile, acc, 64, offset)


def total_kernel(parts, odd, out):
    first, second = [parts[0, pl.ds(k, 32, stride=2), :] + parts[1, pl.ds(k, 32, stride=2), :] for k in range(2)]
    out[...] = jnp.where(odd[...] == 0, first, second)[:, None, :]


def last_kernel(parts, base, out):
    out[...] = EPS * (base[...] - jnp.log(jnp.sum(parts[...], axis=0)))


def call(kernel, kinds, outs, scratch=()):
    specs = [pl.BlockSpec(memory_space=SMEM if kind == "s" else VMEM) for kind in kinds]
    out_specs = [pl.BlockSpec(memory_space=VMEM) for _ in outs]
    shapes = [jax.ShapeDtypeStruct(shape, dtype) for shape, dtype in outs]
    single = len(outs) == 1
    return pl.pallas_call(
        kernel,
        in_specs=specs,
        out_specs=out_specs[0] if single else out_specs,
        out_shape=shapes[0] if single else shapes,
        scratch_shapes=list(scratch),
        compiler_params=pltpu.CompilerParams(vmem_limit_bytes=VMEM_LIMIT),
        name=kernel.__name__,
    )


def columns_of(blocks):
    return [VMEM((blocks * 4, BLK), f32), VMEM((blocks // 16, BLK, BLK), bf16)]


def accumulators(owners, number):
    return [VMEM(((owners + 1) * 8, BLK), f32) for _ in range(number)]


def on_device(source_cells, target_cells, start, source_logmass, target_logmass, pair_src, pair_tgt, pair_count):
    ring = [[z * 4 + r for z in range(16)] for r in range(4)]
    chips = [[z * 4 + r for r in range(4)] for z in range(16)]
    cores = [[i, i + 1] for i in range(0, 64, 2)]
    halves = [[2 * i + c for i in range(32)] for c in range(2)]
    to_core = [(i, i ^ 1) for i in range(64)]
    to_chip = [(i, i ^ 2) for i in range(64)]

    source_mass = source_logmass.reshape(-1, BLK)
    target_mass = target_logmass.reshape(-1, BLK)

    mine = target_cells.T
    own = lax.all_to_all(jnp.broadcast_to(mine[None], (16, DIM, BLK)), "src", 0, 0, axis_index_groups=ring)
    other = lax.ppermute(own, "src", to_chip)
    core = lax.ppermute(own, "src", to_core)
    sources = source_cells.T
    table = ((8, BLK), jnp.int32)
    rows, norms, hot, info_s, info_t = call(
        prepare_kernel,
        "vvvv",
        [((128, BLK, BLK), bf16), ((128, BLK), f32), ((16, DIM, BLK), bf16), table, table],
    )(sources, pair_src.reshape(1, -1), pair_tgt.reshape(1, -1), pair_count)
    other, hot = lax.optimization_barrier((other, hot))
    both = lax.ppermute(other, "src", to_core)

    parts, target_rows, targets = call(
        first_kernel,
        "svvvvvvv",
        [((8, 128, BLK), f32), ((64, BLK, BLK), bf16), ((64, DIM, BLK), bf16)],
        [VMEM((64, BLK), f32)] + columns_of(64) + accumulators(128, 2 * WAYS),
    )(info_s, sources, own, core, other, both, start.reshape(-1, BLK), hot)
    parts = lax.all_to_all(parts, "tgt", 0, 0)
    lse, first_u = call(
        second_kernel,
        "svvvvv",
        [((4, 16, BLK), f32), ((128, BLK), f32)],
        columns_of(128) + accumulators(64, 2 * WAYS),
    )(info_t, rows, targets, parts, source_mass, hot)
    lse = lax.all_to_all(lse, "src", 0, 0, axis_index_groups=chips)
    lse = call(group_kernel, "v", [((16, 16, BLK), f32)])(lse)
    lse = lax.all_to_all(lse, "src", 0, 0, axis_index_groups=ring)
    lse = call(ring_kernel, "v", [((16, BLK), f32)])(lse)
    lse = lax.all_gather(lse, "src", axis=0, axis_index_groups=chips, tiled=True)
    parts, first_v, base = call(
        third_kernel,
        "svvvvvvv",
        [((8, 128, BLK), f32), ((64, BLK), f32), ((1, BLK), f32)],
        columns_of(64) + accumulators(128, 2),
    )(info_s, sources, target_rows, lse, target_mass, first_u, hot, mine)
    parts = lax.all_to_all(parts, "tgt", 0, 0)
    sums, last_u, odd = call(
        fourth_kernel,
        "svvvvvvvv",
        [((64, BLK), f32), ((128, BLK), f32), ((32, BLK), jnp.int32)],
        columns_of(128) + accumulators(64, 2),
    )(info_t, rows, targets, parts, source_mass, first_u, first_v, norms, hot)
    sums = lax.all_gather(sums, "src", axis=0, axis_index_groups=cores)
    sums = call(total_kernel, "vv", [((32, 1, BLK), f32)])(sums, odd)
    sums = lax.all_to_all(sums, "src", 0, 0, axis_index_groups=halves)
    last_v = call(last_kernel, "vv", [((1, BLK), f32)])(sums, base)
    return last_u.reshape(-1), last_v.reshape(-1)


def solution(mesh):
    in_specs = (
        P("src", None),
        P(("tgt", "src"), None),
        P("tgt"),
        P("src"),
        P("tgt"),
        P("src", "tgt", None),
        P("src", "tgt", None),
        P("src", "tgt"),
    )
    out_specs = (P("src"), P(("tgt", "src")))
    return jax.shard_map(
        on_device, mesh=mesh, in_specs=in_specs, out_specs=out_specs, check_vma=False
    )
```

```python
import functools

import jax
import jax.numpy as jnp
from jax import lax
from jax.experimental import pallas as pl
from jax.experimental.pallas import tpu as pltpu
from jax.sharding import PartitionSpec as P

DIM = 64
BLK = 128
EPS = 0.1
SCALE = 2.0 / (DIM * EPS)
LOG2E = 1.4426950408889634
LN2 = 0.6931471805599453
KAPPA = SCALE * LOG2E
LOWEST = -1e30
LEAST, MOST = 2.0**-80, 2.0**120
LIFT = 100.0
OWNER = 20
VMEM_LIMIT = 16 * 1024 * 1024
STEP_BITS = 6
UNROLL = 1 << STEP_BITS
VMEM = pltpu.VMEM
SMEM = pltpu.SMEM
bf16 = jnp.bfloat16
f32 = jnp.float32


def block_of(n):
    return pl.ds(pl.multiple_of(n * BLK, BLK), BLK)


def as_rows(block):
    return jnp.concatenate([block, jnp.zeros((BLK - DIM, BLK), bf16)], axis=0).T


def norm_row(block):
    x = block.astype(f32)
    return jnp.sum(x * x, axis=0, keepdims=True)


def spread(potential, columns_ref, extra_ref):
    blocks = potential.shape[0]
    beta = potential * (1.0 / SCALE)
    hi = beta.astype(bf16).astype(f32)
    rest = beta - hi
    mid = rest.astype(bf16).astype(f32)
    for s, part in enumerate((hi, mid, rest - mid, jnp.zeros_like(hi))):
        columns_ref[pl.ds(s, blocks, stride=4), :] = part
    for g in range(blocks // 16):
        half = columns_ref[g * 64 : g * 64 + 64, :]
        extra_ref[g] = jnp.concatenate([jnp.zeros_like(half), half], axis=0).T.astype(bf16)


def pair_tile(x_ref, extra_ref, hot_ref, x_place, x_id, other_block):
    left = x_ref[x_place] + extra_ref[x_id >> 4]
    right = jnp.concatenate([other_block, hot_ref[x_id & 15]], axis=0)
    return jnp.dot(left, right, preferred_element_type=f32).reshape(16, 8, BLK)


def over_pairs(info, work, bits=STEP_BITS):
    def group(n, carry):
        row, first = 1 + (n >> (7 - bits)), (n << bits) & 127
        work([info[row, first + q] for q in range(1 << bits)])
        return carry

    lax.fori_loop(0, (info[0, 0] + ((1 << bits) - 1)) >> bits, group, 0)


def owner_rows(code):
    return pl.ds(pl.multiple_of(code >> OWNER, 8), 8)


def strided(acc, g):
    return [acc[pl.ds(g * 64 + s, 8, stride=8), :] for s in range(8)]


def stable_lse(info, tile, top, total, owners):
    top[...] = jnp.full(top.shape, LOWEST, f32)
    total[...] = jnp.zeros(total.shape, f32)

    def work(slots):
        stats = []
        for s in slots:
            z = tile(s)
            most = jnp.max(z, axis=0)
            stats.append((most, jnp.sum(jnp.exp2((z - most[None]) * KAPPA), axis=0)))
        for s, (most, part) in zip(slots, stats):
            rows = owner_rows(s)
            old = top[rows, :]
            new = jnp.maximum(old, most)
            total[rows, :] = total[rows, :] * jnp.exp2((old - new) * KAPPA) + part * jnp.exp2((most - new) * KAPPA)
            top[rows, :] = new

    over_pairs(info, work, 3)
    out = []
    for g in range(owners // 8):
        rows = strided(top, g)
        most = functools.reduce(jnp.maximum, rows)
        parts = [p * jnp.exp2((r - most) * KAPPA) for r, p in zip(rows, strided(total, g))]
        whole = functools.reduce(jnp.add, parts)
        out.append(jnp.where(whole > 0.0, most * SCALE + jnp.log(jnp.maximum(whole, 1e-30)), LOWEST))
    return jnp.concatenate(out, axis=0)


def plain_sum(info, tile, total, owners, offset, seen=None):
    total[...] = jnp.zeros(total.shape, f32)
    if seen is not None:
        seen[...] = jnp.zeros(seen.shape, f32)

    def work(slots):
        parts = []
        for s in slots:
            parts.append(jnp.sum(jnp.exp2(tile(s) * KAPPA + offset[owner_rows(s), :][None]), axis=0))
        for s, part in zip(slots, parts):
            rows = owner_rows(s)
            total[rows, :] = total[rows, :] + part
            if seen is not None:
                seen[rows, :] = jnp.ones((8, BLK), f32)

    over_pairs(info, work)
    return jnp.concatenate([functools.reduce(jnp.add, strided(total, g)) for g in range(owners // 8)], axis=0)


def guarded_lse(info, tile, accs, owners, values, offset, write):
    total_ref, seen_ref = accs
    repeat_rows(values, offset)
    total = plain_sum(info, tile, total_ref, owners, offset, seen_ref)
    seen = seen_ref[pl.ds(0, owners, stride=8), :] > 0.0
    fine = (total >= LEAST) & (total <= MOST)
    write(jnp.where(seen, jnp.log(jnp.where(fine, total, 1.0)) - values * LN2, LOWEST))
    lost = jnp.max(jnp.where(seen & jnp.logical_not(fine), 1.0, 0.0))

    @pl.when(lost > 0.0)
    def again():
        write(stable_lse(info, tile, total_ref, seen_ref, owners))


def repeat_rows(values, offset):
    owners = values.shape[0]
    for k in range(8):
        offset[pl.ds(k, owners, stride=8), :] = values
    offset[pl.ds(owners * 8, 8), :] = jnp.zeros((8, BLK), f32)


def by_source(targets, sources, extra, hot):
    def tile(code):
        at = pl.multiple_of(code & 0x3F80, BLK)
        return pair_tile(targets, extra, hot, (code >> 14) & 63, code & 63, sources[:, pl.ds(at, BLK)])

    return tile


def by_target(sources, targets, extra, hot):
    def tile(code):
        s = code & 127
        return pair_tile(sources, extra, hot, s, s, targets[(code >> 14) & 63])

    return tile


def prepare_kernel(sources, pair_src, pair_tgt, pair_count, rows, norms, hot, by_src, by_tgt):
    me = lax.axis_index("src")
    lane = lax.broadcasted_iota(jnp.int32, (1, BLK), 1)
    count = jnp.broadcast_to(pair_count[...], (1, BLK))
    steps = (count + (UNROLL - 1)) >> STEP_BITS
    for k, value in enumerate((me, me & 1, me & 3, steps, count)):
        head = value if k == 0 else jnp.where(lane == 4 - k, value, head)
    by_src[0:1, :] = jnp.broadcast_to(head, (1, BLK))
    by_tgt[0:1, :] = jnp.broadcast_to(head, (1, BLK))
    for half in range(2):
        used = lane + half * BLK < count
        part = slice(half * BLK, (half + 1) * BLK)
        s, t = jnp.where(used, pair_src[:, part], 0), jnp.where(used, pair_tgt[:, part], 0)
        place = (((t ^ me) & 3) << 4) + (t >> 2)
        by_src[half + 1 : half + 2, :] = t + (s << 7) + (place << 14) + (jnp.where(used, s, 128) << (OWNER + 3))
        by_tgt[half + 1 : half + 2, :] = s + (place << 14) + (jnp.where(used, t, 64) << (OWNER + 3))
    line = lax.broadcasted_iota(jnp.int32, (DIM, BLK), 0)
    for r in range(16):
        hot[r] = jnp.where((line >= 4 * r) & (line < 4 * r + 3), 1.0, 0.0).astype(bf16)
    for b in range(128):
        block = sources[:, b * BLK : b * BLK + BLK]
        rows[b] = as_rows(block)
        norms[b : b + 1, :] = norm_row(block)


def merge_lse(parts_ref):
    top = jnp.max(parts_ref[...], axis=0)
    total = jnp.sum(jnp.exp(parts_ref[...] - top[None]), axis=0)
    return top + jnp.log(total)


def first_kernel(
    info, sources, own, core, other, both, start, source_norms, hot,
    out, rows, targets, potential, norms, columns, extra, offset, *accs,
):
    mine = info[0, 2]
    for d, part in enumerate((own, core, other, both)):
        for z in range(16):
            block = part[z]
            targets[d * 16 + z] = block
            rows[d * 16 + z] = as_rows(block)
            norms[pl.ds(z * 4 + (d ^ mine), 1), :] = norm_row(block)
    new = start[...] * (1.0 / EPS) - norms[...] * (SCALE / 2)
    potential[...] = new
    spread(new, columns, extra)
    tile = by_source(rows, sources, extra, hot)

    def write(lse):
        for k in range(8):
            out[k] = lse

    guarded_lse(info, tile, accs, 128, source_norms[...] * (-LOG2E * SCALE / 2), offset, write)


def second_kernel(info, rows, targets, parts, mass, former, hot, out, potential, columns, extra, offset, *accs):
    new = mass[...] - merge_lse(parts)
    potential[...] = new
    spread(new, columns, extra)
    tile = by_target(rows, targets, extra, hot)

    def write(lse):
        for k in range(4):
            out[k] = lse[16 * k : 16 * k + 16]

    guarded_lse(info, tile, accs, 64, former[...] * LOG2E + LIFT, offset, write)


def group_kernel(parts, out):
    lse = merge_lse(parts)
    for k in range(16):
        out[k] = lse


def ring_kernel(parts, out):
    out[...] = merge_lse(parts)


def third_kernel(
    info, sources, rows, lse, mass, reference, hot, mine, out, potential, base, columns, extra, offset, acc
):
    me = info[0, 4]
    new = mass[...] - lse[...]
    potential[...] = new
    base[...] = potential[pl.ds(me, 1), :] + mass[pl.ds(me, 1), :] + norm_row(mine[...]) * (SCALE / 2)
    spread(new, columns, extra)
    repeat_rows(reference[...] * LOG2E, offset)
    tile = by_source(rows, sources, extra, hot)
    total = plain_sum(info, tile, acc, 128, offset)
    for k in range(8):
        out[k] = total


def fourth_kernel(
    info, rows, targets, parts, mass, former, reference, norms, hot,
    out, final, odd, columns, extra, offset, acc,
):
    new = former[...] + mass[...] - jnp.log(jnp.sum(parts[...], axis=0))
    spread(new, columns, extra)
    final[...] = EPS * (new + norms[...] * (SCALE / 2))
    odd[...] = jnp.full(odd.shape, info[0, 3], jnp.int32)
    repeat_rows(reference[...] * LOG2E, offset)
    tile = by_target(rows, targets, extra, hot)
    out[...] = plain_sum(info, tile, acc, 64, offset)


def total_kernel(parts, odd, out):
    first, second = [parts[0, pl.ds(k, 32, stride=2), :] + parts[1, pl.ds(k, 32, stride=2), :] for k in range(2)]
    out[...] = jnp.where(odd[...] == 0, first, second)[:, None, :]


def last_kernel(parts, base, out):
    out[...] = EPS * (base[...] - jnp.log(jnp.sum(parts[...], axis=0)))


def call(kernel, kinds, outs, scratch=()):
    specs = [pl.BlockSpec(memory_space=SMEM if kind == "s" else VMEM) for kind in kinds]
    out_specs = [pl.BlockSpec(memory_space=VMEM) for _ in outs]
    shapes = [jax.ShapeDtypeStruct(shape, dtype) for shape, dtype in outs]
    single = len(outs) == 1
    return pl.pallas_call(
        kernel,
        in_specs=specs,
        out_specs=out_specs[0] if single else out_specs,
        out_shape=shapes[0] if single else shapes,
        scratch_shapes=list(scratch),
        compiler_params=pltpu.CompilerParams(vmem_limit_bytes=VMEM_LIMIT),
        name=kernel.__name__,
    )


def columns_of(blocks):
    return [VMEM((blocks * 4, BLK), f32), VMEM((blocks // 16, BLK, BLK), bf16)]


def accumulators(owners, number):
    return [VMEM(((owners + 1) * 8, BLK), f32) for _ in range(number)]


def on_device(source_cells, target_cells, start, source_logmass, target_logmass, pair_src, pair_tgt, pair_count):
    ring = [[z * 4 + r for z in range(16)] for r in range(4)]
    chips = [[z * 4 + r for r in range(4)] for z in range(16)]
    cores = [[i, i + 1] for i in range(0, 64, 2)]
    halves = [[2 * i + c for i in range(32)] for c in range(2)]
    to_core = [(i, i ^ 1) for i in range(64)]
    to_chip = [(i, i ^ 2) for i in range(64)]

    source_mass = source_logmass.reshape(-1, BLK)
    target_mass = target_logmass.reshape(-1, BLK)

    mine = target_cells.T
    own = lax.all_to_all(jnp.broadcast_to(mine[None], (16, DIM, BLK)), "src", 0, 0, axis_index_groups=ring)
    other = lax.ppermute(own, "src", to_chip)
    core = lax.ppermute(own, "src", to_core)
    sources = source_cells.T
    table = ((8, BLK), jnp.int32)
    rows, norms, hot, info_s, info_t = call(
        prepare_kernel,
        "vvvv",
        [((128, BLK, BLK), bf16), ((128, BLK), f32), ((16, DIM, BLK), bf16), table, table],
    )(sources, pair_src.reshape(1, -1), pair_tgt.reshape(1, -1), pair_count)
    other, hot = lax.optimization_barrier((other, hot))
    both = lax.ppermute(other, "src", to_core)

    parts, target_rows, targets, start_v = call(
        first_kernel,
        "svvvvvvvv",
        [((8, 128, BLK), f32), ((64, BLK, BLK), bf16), ((64, DIM, BLK), bf16), ((64, BLK), f32)],
        [VMEM((64, BLK), f32)] + columns_of(64) + accumulators(128, 3),
    )(info_s, sources, own, core, other, both, start.reshape(-1, BLK), norms, hot)
    parts = lax.all_to_all(parts, "tgt", 0, 0)
    lse, first_u = call(
        second_kernel,
        "svvvvvv",
        [((4, 16, BLK), f32), ((128, BLK), f32)],
        columns_of(128) + accumulators(64, 3),
    )(info_t, rows, targets, parts, source_mass, start_v, hot)
    lse = lax.all_to_all(lse, "src", 0, 0, axis_index_groups=chips)
    lse = call(group_kernel, "v", [((16, 16, BLK), f32)])(lse)
    lse = lax.all_to_all(lse, "src", 0, 0, axis_index_groups=ring)
    lse = call(ring_kernel, "v", [((16, BLK), f32)])(lse)
    lse = lax.all_gather(lse, "src", axis=0, axis_index_groups=chips, tiled=True)
    parts, first_v, base = call(
        third_kernel,
        "svvvvvvv",
        [((8, 128, BLK), f32), ((64, BLK), f32), ((1, BLK), f32)],
        columns_of(64) + accumulators(128, 2),
    )(info_s, sources, target_rows, lse, target_mass, first_u, hot, mine)
    parts = lax.all_to_all(parts, "tgt", 0, 0)
    sums, last_u, odd = call(
        fourth_kernel,
        "svvvvvvvv",
        [((64, BLK), f32), ((128, BLK), f32), ((32, BLK), jnp.int32)],
        columns_of(128) + accumulators(64, 2),
    )(info_t, rows, targets, parts, source_mass, first_u, first_v, norms, hot)
    sums = lax.all_gather(sums, "src", axis=0, axis_index_groups=cores)
    sums = call(total_kernel, "vv", [((32, 1, BLK), f32)])(sums, odd)
    sums = lax.all_to_all(sums, "src", 0, 0, axis_index_groups=halves)
    last_v = call(last_kernel, "vv", [((1, BLK), f32)])(sums, base)
    return last_u.reshape(-1), last_v.reshape(-1)


def solution(mesh):
    in_specs = (
        P("src", None),
        P(("tgt", "src"), None),
        P("tgt"),
        P("src"),
        P("tgt"),
        P("src", "tgt", None),
        P("src", "tgt", None),
        P("src", "tgt"),
    )
    out_specs = (P("src"), P(("tgt", "src")))
    return jax.shard_map(
        on_device, mesh=mesh, in_specs=in_specs, out_specs=out_specs, check_vma=False
    )
```

```python
import functools

import jax
import jax.numpy as jnp
from jax import lax
from jax.experimental import pallas as pl
from jax.experimental.pallas import tpu as pltpu
from jax.sharding import PartitionSpec as P

DIM = 64
BLK = 128
EPS = 0.1
SCALE = 2.0 / (DIM * EPS)
LOG2E = 1.4426950408889634
LN2 = 0.6931471805599453
KAPPA = SCALE * LOG2E
LOWEST = -1e30
LEAST, MOST = 2.0**-80, 2.0**120
LIFT = 100.0
OWNER = 20
VMEM_LIMIT = 16 * 1024 * 1024
STEP_BITS = 6
UNROLL = 1 << STEP_BITS
VMEM = pltpu.VMEM
SMEM = pltpu.SMEM
bf16 = jnp.bfloat16
f32 = jnp.float32


def block_of(n):
    return pl.ds(pl.multiple_of(n * BLK, BLK), BLK)


def as_rows(block):
    return jnp.concatenate([block, jnp.zeros((BLK - DIM, BLK), bf16)], axis=0).T


def norm_row(block):
    x = block.astype(f32)
    return jnp.sum(x * x, axis=0, keepdims=True)


def spread(potential, columns_ref, extra_ref):
    blocks = potential.shape[0]
    beta = potential * (1.0 / SCALE)
    hi = beta.astype(bf16).astype(f32)
    rest = beta - hi
    mid = rest.astype(bf16).astype(f32)
    for s, part in enumerate((hi, mid, rest - mid, jnp.zeros_like(hi))):
        columns_ref[pl.ds(s, blocks, stride=4), :] = part
    for g in range(blocks // 16):
        half = columns_ref[g * 64 : g * 64 + 64, :]
        extra_ref[g] = jnp.concatenate([jnp.zeros_like(half), half], axis=0).T.astype(bf16)


def pair_tile(x_ref, extra_ref, hot_ref, x_place, x_id, other_block):
    left = x_ref[x_place] + extra_ref[x_id >> 4]
    right = jnp.concatenate([other_block, hot_ref[x_id & 15]], axis=0)
    return jnp.dot(left, right, preferred_element_type=f32).reshape(16, 8, BLK)


def over_pairs(info, work, bits=STEP_BITS):
    def group(n, carry):
        row, first = 1 + (n >> (7 - bits)), (n << bits) & 127
        work([info[row, first + q] for q in range(1 << bits)])
        return carry

    lax.fori_loop(0, (info[0, 0] + ((1 << bits) - 1)) >> bits, group, 0)


def owner_rows(code):
    return pl.ds(pl.multiple_of(code >> OWNER, 8), 8)


def strided(acc, g):
    return [acc[pl.ds(g * 64 + s, 8, stride=8), :] for s in range(8)]


def stable_lse(info, tile, top, total, owners):
    top[...] = jnp.full(top.shape, LOWEST, f32)
    total[...] = jnp.zeros(total.shape, f32)

    def work(slots):
        stats = []
        for s in slots:
            z = tile(s)
            most = jnp.max(z, axis=0)
            stats.append((most, jnp.sum(jnp.exp2((z - most[None]) * KAPPA), axis=0)))
        for s, (most, part) in zip(slots, stats):
            rows = owner_rows(s)
            old = top[rows, :]
            new = jnp.maximum(old, most)
            total[rows, :] = total[rows, :] * jnp.exp2((old - new) * KAPPA) + part * jnp.exp2((most - new) * KAPPA)
            top[rows, :] = new

    over_pairs(info, work, 3)
    out = []
    for g in range(owners // 8):
        rows = strided(top, g)
        most = functools.reduce(jnp.maximum, rows)
        parts = [p * jnp.exp2((r - most) * KAPPA) for r, p in zip(rows, strided(total, g))]
        whole = functools.reduce(jnp.add, parts)
        out.append(jnp.where(whole > 0.0, most * SCALE + jnp.log(jnp.maximum(whole, 1e-30)), LOWEST))
    return jnp.concatenate(out, axis=0)


def plain_sum(info, tile, total, owners, offset, seen=None):
    total[...] = jnp.zeros(total.shape, f32)
    if seen is not None:
        seen[...] = jnp.zeros(seen.shape, f32)

    def work(slots):
        parts = []
        for s in slots:
            parts.append(jnp.sum(jnp.exp2(tile(s) * KAPPA + offset[owner_rows(s), :][None]), axis=0))
        for s, part in zip(slots, parts):
            rows = owner_rows(s)
            total[rows, :] = total[rows, :] + part
            if seen is not None:
                seen[rows, :] = jnp.ones((8, BLK), f32)

    over_pairs(info, work)
    return jnp.concatenate([functools.reduce(jnp.add, strided(total, g)) for g in range(owners // 8)], axis=0)


def guarded_lse(info, tile, accs, owners, values, offset, write):
    total_ref, seen_ref = accs
    repeat_rows(values, offset)
    total = plain_sum(info, tile, total_ref, owners, offset, seen_ref)
    seen = seen_ref[pl.ds(0, owners, stride=8), :] > 0.0
    fine = (total >= LEAST) & (total <= MOST)
    write(jnp.where(seen, jnp.log(jnp.where(fine, total, 1.0)) - values * LN2, LOWEST))
    lost = jnp.max(jnp.where(seen & jnp.logical_not(fine), 1.0, 0.0))

    @pl.when(lost > 0.0)
    def again():
        write(stable_lse(info, tile, total_ref, seen_ref, owners))


def repeat_rows(values, offset):
    owners = values.shape[0]
    for k in range(8):
        offset[pl.ds(k, owners, stride=8), :] = values
    offset[pl.ds(owners * 8, 8), :] = jnp.zeros((8, BLK), f32)


def by_source(targets, sources, extra, hot):
    def tile(code):
        at = pl.multiple_of(code & 0x3F80, BLK)
        return pair_tile(targets, extra, hot, (code >> 14) & 63, code & 63, sources[:, pl.ds(at, BLK)])

    return tile


def by_target(sources, targets, extra, hot):
    def tile(code):
        s = code & 127
        return pair_tile(sources, extra, hot, s, s, targets[(code >> 14) & 63])

    return tile


def prepare_kernel(sources, pair_src, pair_tgt, pair_count, rows, norms, hot, by_src, by_tgt):
    me = lax.axis_index("src")
    lane = lax.broadcasted_iota(jnp.int32, (1, BLK), 1)
    count = jnp.broadcast_to(pair_count[...], (1, BLK))
    by_src[0:1, :] = count
    by_tgt[0:1, :] = count
    for half in range(2):
        used = lane + half * BLK < count
        part = slice(half * BLK, (half + 1) * BLK)
        s, t = jnp.where(used, pair_src[:, part], 0), jnp.where(used, pair_tgt[:, part], 0)
        place = (((t ^ (me & 2)) & 3) << 4) + (t >> 2)
        by_src[half + 1 : half + 2, :] = t + (s << 7) + (place << 14) + (jnp.where(used, s, 128) << (OWNER + 3))
        by_tgt[half + 1 : half + 2, :] = s + (place << 14) + (jnp.where(used, t, 64) << (OWNER + 3))
    line = lax.broadcasted_iota(jnp.int32, (DIM, BLK), 0)
    for r in range(16):
        hot[r] = jnp.where((line >= 4 * r) & (line < 4 * r + 3), 1.0, 0.0).astype(bf16)
    for b in range(128):
        block = sources[:, b * BLK : b * BLK + BLK]
        rows[b] = as_rows(block)
        norms[b : b + 1, :] = norm_row(block)


def merge_lse(parts_ref):
    top = jnp.max(parts_ref[...], axis=0)
    total = jnp.sum(jnp.exp(parts_ref[...] - top[None]), axis=0)
    return top + jnp.log(total)


def first_kernel(
    words, sources, own, other, start, source_norms, hot,
    out, rows, targets, potential, info, arrival, norms, columns, extra, offset, *accs,
):
    coming = pltpu.make_async_copy(words, info, arrival)
    coming.start()
    mine = lax.axis_index("src") & 2
    for d in range(4):
        for z in range(16):
            block = (own, other)[d >> 1][d & 1, z]
            targets[d * 16 + z] = block
            rows[d * 16 + z] = as_rows(block)
            norms[pl.ds(z * 4 + (d ^ mine), 1), :] = norm_row(block)
    new = start[...] * (1.0 / EPS) - norms[...] * (SCALE / 2)
    potential[...] = new
    spread(new, columns, extra)
    coming.wait()
    tile = by_source(rows, sources, extra, hot)

    def write(lse):
        for k in range(8):
            out[k] = lse

    guarded_lse(info, tile, accs, 128, source_norms[...] * (-LOG2E * SCALE / 2), offset, write)


def second_kernel(
    words, rows, targets, parts, mass, former, hot, out, potential, info, arrival, columns, extra, offset, *accs
):
    coming = pltpu.make_async_copy(words, info, arrival)
    coming.start()
    new = mass[...] - merge_lse(parts)
    potential[...] = new
    spread(new, columns, extra)
    coming.wait()
    tile = by_target(rows, targets, extra, hot)

    def write(lse):
        for k in range(4):
            out[k] = lse[16 * k : 16 * k + 16]

    guarded_lse(info, tile, accs, 64, former[...] * LOG2E + LIFT, offset, write)


def group_kernel(parts, out):
    lse = merge_lse(parts)
    for k in range(16):
        out[k] = lse


def ring_kernel(parts, out):
    out[...] = merge_lse(parts)


def third_kernel(
    words, sources, rows, lse, mass, reference, hot, mine,
    out, potential, base, info, arrival, columns, extra, offset, acc,
):
    coming = pltpu.make_async_copy(words, info, arrival)
    coming.start()
    me = lax.axis_index("src")
    new = mass[...] - lse[...]
    potential[...] = new
    base[...] = potential[pl.ds(me, 1), :] + mass[pl.ds(me, 1), :] + norm_row(mine[...]) * (SCALE / 2)
    spread(new, columns, extra)
    repeat_rows(reference[...] * LOG2E, offset)
    coming.wait()
    tile = by_source(rows, sources, extra, hot)
    total = plain_sum(info, tile, acc, 128, offset)
    for k in range(8):
        out[k] = total


def fourth_kernel(
    words, rows, targets, parts, mass, former, reference, norms, hot,
    out, final, odd, info, arrival, columns, extra, offset, acc,
):
    coming = pltpu.make_async_copy(words, info, arrival)
    coming.start()
    new = former[...] + mass[...] - jnp.log(jnp.sum(parts[...], axis=0))
    spread(new, columns, extra)
    final[...] = EPS * (new + norms[...] * (SCALE / 2))
    odd[...] = jnp.full(odd.shape, lax.axis_index("src") & 1, jnp.int32)
    repeat_rows(reference[...] * LOG2E, offset)
    coming.wait()
    tile = by_target(rows, targets, extra, hot)
    out[...] = plain_sum(info, tile, acc, 64, offset)


def total_kernel(parts, odd, out):
    first, second = [parts[0, pl.ds(k, 32, stride=2), :] + parts[1, pl.ds(k, 32, stride=2), :] for k in range(2)]
    out[...] = jnp.where(odd[...] == 0, first, second)[:, None, :]


def last_kernel(parts, base, out):
    out[...] = EPS * (base[...] - jnp.log(jnp.sum(parts[...], axis=0)))


def call(kernel, inputs, outs, scratch=()):
    out_specs = [pl.BlockSpec(memory_space=VMEM) for _ in outs]
    shapes = [jax.ShapeDtypeStruct(shape, dtype) for shape, dtype in outs]
    single = len(outs) == 1
    return pl.pallas_call(
        kernel,
        in_specs=[pl.BlockSpec(memory_space=VMEM) for _ in range(inputs)],
        out_specs=out_specs[0] if single else out_specs,
        out_shape=shapes[0] if single else shapes,
        scratch_shapes=list(scratch),
        compiler_params=pltpu.CompilerParams(vmem_limit_bytes=VMEM_LIMIT),
        name=kernel.__name__,
    )


WORDS = [SMEM((8, BLK), jnp.int32), pltpu.SemaphoreType.DMA]


def columns_of(blocks):
    return [VMEM((blocks * 4, BLK), f32), VMEM((blocks // 16, BLK, BLK), bf16)]


def accumulators(owners, number):
    return [VMEM(((owners + 1) * 8, BLK), f32) for _ in range(number)]


def on_device(source_cells, target_cells, start, source_logmass, target_logmass, pair_src, pair_tgt, pair_count):
    ring = [[z * 4 + r for z in range(16)] for r in range(4)]
    chips = [[z * 4 + r for r in range(4)] for z in range(16)]
    cores = [[i, i + 1] for i in range(0, 64, 2)]
    halves = [[2 * i + c for i in range(32)] for c in range(2)]
    to_chip = [(i, i ^ 2) for i in range(64)]

    source_mass = source_logmass.reshape(-1, BLK)
    target_mass = target_logmass.reshape(-1, BLK)

    mine = target_cells.T
    own = lax.all_to_all(jnp.broadcast_to(mine[None], (16, DIM, BLK)), "src", 0, 0, axis_index_groups=ring)
    other = lax.ppermute(own, "src", to_chip)
    own = lax.all_gather(own, "src", axis=0, axis_index_groups=cores)
    sources = source_cells.T
    table = ((8, BLK), jnp.int32)
    rows, norms, hot, info_s, info_t = call(
        prepare_kernel,
        4,
        [((128, BLK, BLK), bf16), ((128, BLK), f32), ((16, DIM, BLK), bf16), table, table],
    )(sources, pair_src.reshape(1, -1), pair_tgt.reshape(1, -1), pair_count)
    other, hot = lax.optimization_barrier((other, hot))
    other = lax.all_gather(other, "src", axis=0, axis_index_groups=cores)

    parts, target_rows, targets, start_v = call(
        first_kernel,
        7,
        [((8, 128, BLK), f32), ((64, BLK, BLK), bf16), ((64, DIM, BLK), bf16), ((64, BLK), f32)],
        WORDS + [VMEM((64, BLK), f32)] + columns_of(64) + accumulators(128, 3),
    )(info_s, sources, own, other, start.reshape(-1, BLK), norms, hot)
    parts = lax.all_to_all(parts, "tgt", 0, 0)
    lse, first_u = call(
        second_kernel,
        7,
        [((4, 16, BLK), f32), ((128, BLK), f32)],
        WORDS + columns_of(128) + accumulators(64, 3),
    )(info_t, rows, targets, parts, source_mass, start_v, hot)
    lse = lax.all_to_all(lse, "src", 0, 0, axis_index_groups=chips)
    lse = call(group_kernel, 1, [((16, 16, BLK), f32)])(lse)
    lse = lax.all_to_all(lse, "src", 0, 0, axis_index_groups=ring)
    lse = call(ring_kernel, 1, [((16, BLK), f32)])(lse)
    lse = lax.all_gather(lse, "src", axis=0, axis_index_groups=chips, tiled=True)
    parts, first_v, base = call(
        third_kernel,
        8,
        [((8, 128, BLK), f32), ((64, BLK), f32), ((1, BLK), f32)],
        WORDS + columns_of(64) + accumulators(128, 2),
    )(info_s, sources, target_rows, lse, target_mass, first_u, hot, mine)
    parts = lax.all_to_all(parts, "tgt", 0, 0)
    sums, last_u, odd = call(
        fourth_kernel,
        9,
        [((64, BLK), f32), ((128, BLK), f32), ((32, BLK), jnp.int32)],
        WORDS + columns_of(128) + accumulators(64, 2),
    )(info_t, rows, targets, parts, source_mass, first_u, first_v, norms, hot)
    sums = lax.all_gather(sums, "src", axis=0, axis_index_groups=cores)
    sums = call(total_kernel, 2, [((32, 1, BLK), f32)])(sums, odd)
    sums = lax.all_to_all(sums, "src", 0, 0, axis_index_groups=halves)
    last_v = call(last_kernel, 2, [((1, BLK), f32)])(sums, base)
    return last_u.reshape(-1), last_v.reshape(-1)


def solution(mesh):
    in_specs = (
        P("src", None),
        P(("tgt", "src"), None),
        P("tgt"),
        P("src"),
        P("tgt"),
        P("src", "tgt", None),
        P("src", "tgt", None),
        P("src", "tgt"),
    )
    out_specs = (P("src"), P(("tgt", "src")))
    return jax.shard_map(
        on_device, mesh=mesh, in_specs=in_specs, out_specs=out_specs, check_vma=False
    )
```

```python
import functools

import jax
import jax.numpy as jnp
from jax import lax
from jax.experimental import pallas as pl
from jax.experimental.pallas import tpu as pltpu
from jax.sharding import PartitionSpec as P

DIM = 64
BLK = 128
EPS = 0.1
SCALE = 2.0 / (DIM * EPS)
LOG2E = 1.4426950408889634
LN2 = 0.6931471805599453
KAPPA = SCALE * LOG2E
LOWEST = -1e30
LEAST, MOST = 2.0**-80, 2.0**120
LIFT = 100.0
OWNER = 20
VMEM_LIMIT = 16 * 1024 * 1024
STEP_BITS = 7
UNROLL = 1 << STEP_BITS
VMEM = pltpu.VMEM
SMEM = pltpu.SMEM
bf16 = jnp.bfloat16
f32 = jnp.float32


def block_of(n):
    return pl.ds(pl.multiple_of(n * BLK, BLK), BLK)


def as_rows(block):
    return jnp.concatenate([block, jnp.zeros((BLK - DIM, BLK), bf16)], axis=0).T


def norm_row(block):
    x = block.astype(f32)
    return jnp.sum(x * x, axis=0, keepdims=True)


def spread(potential, columns_ref, extra_ref):
    blocks = potential.shape[0]
    beta = potential * (1.0 / SCALE)
    hi = beta.astype(bf16).astype(f32)
    rest = beta - hi
    mid = rest.astype(bf16).astype(f32)
    for s, part in enumerate((hi, mid, rest - mid, jnp.zeros_like(hi))):
        columns_ref[pl.ds(s, blocks, stride=4), :] = part
    for g in range(blocks // 16):
        half = columns_ref[g * 64 : g * 64 + 64, :]
        extra_ref[g] = jnp.concatenate([jnp.zeros_like(half), half], axis=0).T.astype(bf16)


def pair_tile(x_ref, extra_ref, hot_ref, x_place, x_id, other_block):
    left = x_ref[x_place] + extra_ref[x_id >> 4]
    right = jnp.concatenate([other_block, hot_ref[x_id & 15]], axis=0)
    return jnp.dot(left, right, preferred_element_type=f32).reshape(16, 8, BLK)


def over_pairs(info, work, bits=STEP_BITS):
    def group(n, carry):
        row, first = 1 + (n >> (7 - bits)), (n << bits) & 127
        work([info[row, first + q] for q in range(1 << bits)])
        return carry

    lax.fori_loop(0, (info[0, 0] + ((1 << bits) - 1)) >> bits, group, 0)


def owner_rows(code):
    return pl.ds(pl.multiple_of(code >> OWNER, 8), 8)


def strided(acc, g):
    return [acc[pl.ds(g * 64 + s, 8, stride=8), :] for s in range(8)]


def stable_lse(info, tile, top, total, owners):
    top[...] = jnp.full(top.shape, LOWEST, f32)
    total[...] = jnp.zeros(total.shape, f32)

    def work(slots):
        stats = []
        for s in slots:
            z = tile(s)
            most = jnp.max(z, axis=0)
            stats.append((most, jnp.sum(jnp.exp2((z - most[None]) * KAPPA), axis=0)))
        for s, (most, part) in zip(slots, stats):
            rows = owner_rows(s)
            old = top[rows, :]
            new = jnp.maximum(old, most)
            total[rows, :] = total[rows, :] * jnp.exp2((old - new) * KAPPA) + part * jnp.exp2((most - new) * KAPPA)
            top[rows, :] = new

    over_pairs(info, work, 3)
    out = []
    for g in range(owners // 8):
        rows = strided(top, g)
        most = functools.reduce(jnp.maximum, rows)
        parts = [p * jnp.exp2((r - most) * KAPPA) for r, p in zip(rows, strided(total, g))]
        whole = functools.reduce(jnp.add, parts)
        out.append(jnp.where(whole > 0.0, most * SCALE + jnp.log(jnp.maximum(whole, 1e-30)), LOWEST))
    return jnp.concatenate(out, axis=0)


def plain_sum(info, tile, total, owners, offset, seen=None):
    total[...] = jnp.zeros(total.shape, f32)
    if seen is not None:
        seen[...] = jnp.zeros(seen.shape, f32)

    def work(slots):
        parts = []
        for s in slots:
            parts.append(jnp.sum(jnp.exp2(tile(s) * KAPPA + offset[owner_rows(s), :][None]), axis=0))
        for s, part in zip(slots, parts):
            rows = owner_rows(s)
            total[rows, :] = total[rows, :] + part
            if seen is not None:
                seen[rows, :] = jnp.ones((8, BLK), f32)

    over_pairs(info, work)
    return jnp.concatenate([functools.reduce(jnp.add, strided(total, g)) for g in range(owners // 8)], axis=0)


def guarded_lse(info, tile, accs, owners, values, offset, write):
    total_ref, seen_ref = accs
    repeat_rows(values, offset)
    total = plain_sum(info, tile, total_ref, owners, offset, seen_ref)
    seen = seen_ref[pl.ds(0, owners, stride=8), :] > 0.0
    fine = (total >= LEAST) & (total <= MOST)
    write(jnp.where(seen, jnp.log(jnp.where(fine, total, 1.0)) - values * LN2, LOWEST))
    lost = jnp.max(jnp.where(seen & jnp.logical_not(fine), 1.0, 0.0))

    @pl.when(lost > 0.0)
    def again():
        write(stable_lse(info, tile, total_ref, seen_ref, owners))


def repeat_rows(values, offset):
    owners = values.shape[0]
    for k in range(8):
        offset[pl.ds(k, owners, stride=8), :] = values
    offset[pl.ds(owners * 8, 8), :] = jnp.zeros((8, BLK), f32)


def by_source(targets, sources, extra, hot):
    def tile(code):
        at = pl.multiple_of(code & 0x3F80, BLK)
        return pair_tile(targets, extra, hot, (code >> 14) & 63, code & 63, sources[:, pl.ds(at, BLK)])

    return tile


def by_target(sources, targets, extra, hot):
    def tile(code):
        s = code & 127
        return pair_tile(sources, extra, hot, s, s, targets[(code >> 14) & 63])

    return tile


def prepare_kernel(sources, pair_src, pair_tgt, pair_count, rows, norms, hot, by_src, by_tgt):
    me = lax.axis_index("src")
    lane = lax.broadcasted_iota(jnp.int32, (1, BLK), 1)
    count = jnp.broadcast_to(pair_count[...], (1, BLK))
    by_src[0:1, :] = count
    by_tgt[0:1, :] = count
    for half in range(2):
        used = lane + half * BLK < count
        part = slice(half * BLK, (half + 1) * BLK)
        s, t = jnp.where(used, pair_src[:, part], 0), jnp.where(used, pair_tgt[:, part], 0)
        place = (((t ^ (me & 2)) & 3) << 4) + (t >> 2)
        by_src[half + 1 : half + 2, :] = t + (s << 7) + (place << 14) + (jnp.where(used, s, 128) << (OWNER + 3))
        by_tgt[half + 1 : half + 2, :] = s + (place << 14) + (jnp.where(used, t, 64) << (OWNER + 3))
    line = lax.broadcasted_iota(jnp.int32, (DIM, BLK), 0)
    for r in range(16):
        hot[r] = jnp.where((line >= 4 * r) & (line < 4 * r + 3), 1.0, 0.0).astype(bf16)
    for b in range(128):
        block = sources[:, b * BLK : b * BLK + BLK]
        rows[b] = as_rows(block)
        norms[b : b + 1, :] = norm_row(block)


def merge_lse(parts_ref):
    top = jnp.max(parts_ref[...], axis=0)
    total = jnp.sum(jnp.exp(parts_ref[...] - top[None]), axis=0)
    return top + jnp.log(total)


def first_kernel(
    words, sources, own, other, start, source_norms, hot,
    out, rows, targets, potential, info, arrival, norms, columns, extra, offset, *accs,
):
    coming = pltpu.make_async_copy(words, info, arrival)
    coming.start()
    mine = lax.axis_index("src") & 2
    for d in range(4):
        for z in range(16):
            block = (own, other)[d >> 1][d & 1, z]
            targets[d * 16 + z] = block
            rows[d * 16 + z] = as_rows(block)
            norms[pl.ds(z * 4 + (d ^ mine), 1), :] = norm_row(block)
    new = start[...] * (1.0 / EPS) - norms[...] * (SCALE / 2)
    potential[...] = new
    spread(new, columns, extra)
    coming.wait()
    tile = by_source(rows, sources, extra, hot)

    def write(lse):
        for k in range(8):
            out[k] = lse

    guarded_lse(info, tile, accs, 128, source_norms[...] * (-LOG2E * SCALE / 2), offset, write)


def second_kernel(
    words, rows, targets, parts, mass, former, hot, out, potential, info, arrival, columns, extra, offset, *accs
):
    coming = pltpu.make_async_copy(words, info, arrival)
    coming.start()
    new = mass[...] - merge_lse(parts)
    potential[...] = new
    spread(new, columns, extra)
    coming.wait()
    tile = by_target(rows, targets, extra, hot)

    def write(lse):
        for k in range(4):
            out[k] = lse[16 * k : 16 * k + 16]

    guarded_lse(info, tile, accs, 64, former[...] * LOG2E + LIFT, offset, write)


def group_kernel(parts, out):
    lse = merge_lse(parts)
    for k in range(16):
        out[k] = lse


def ring_kernel(parts, out):
    out[...] = merge_lse(parts)


def third_kernel(
    words, sources, rows, lse, mass, reference, hot, mine,
    out, potential, base, info, arrival, columns, extra, offset, acc,
):
    coming = pltpu.make_async_copy(words, info, arrival)
    coming.start()
    me = lax.axis_index("src")
    new = mass[...] - lse[...]
    potential[...] = new
    base[...] = potential[pl.ds(me, 1), :] + mass[pl.ds(me, 1), :] + norm_row(mine[...]) * (SCALE / 2)
    spread(new, columns, extra)
    repeat_rows(reference[...] * LOG2E, offset)
    coming.wait()
    tile = by_source(rows, sources, extra, hot)
    total = plain_sum(info, tile, acc, 128, offset)
    for k in range(8):
        out[k] = total


def fourth_kernel(
    words, rows, targets, parts, mass, former, reference, norms, hot,
    out, final, odd, info, arrival, held, columns, extra, offset, acc,
):
    coming = pltpu.make_async_copy(words, info, arrival)
    coming.start()
    new = former[...] + mass[...] - jnp.log(jnp.sum(parts[...], axis=0))
    spread(new, columns, extra)
    final[...] = EPS * (new + norms[...] * (SCALE / 2))
    odd[...] = jnp.full(odd.shape, lax.axis_index("src") & 1, jnp.int32)
    repeat_rows(reference[...] * LOG2E, offset)
    coming.wait()
    tile = by_target(rows, targets, extra, hot)
    held[pl.ds(0, 64), :] = plain_sum(info, tile, acc, 64, offset)
    for k in range(2):
        out[k] = held[pl.ds(k, 32, stride=2), :]


def total_kernel(parts, odd, out):
    out[...] = jnp.where(odd[...] == 0, parts[0, 0] + parts[1, 0], parts[0, 1] + parts[1, 1])[:, None, :]


def last_kernel(parts, base, out):
    out[...] = EPS * (base[...] - jnp.log(jnp.sum(parts[...], axis=0)))


def call(kernel, inputs, outs, scratch=()):
    out_specs = [pl.BlockSpec(memory_space=VMEM) for _ in outs]
    shapes = [jax.ShapeDtypeStruct(shape, dtype) for shape, dtype in outs]
    single = len(outs) == 1
    return pl.pallas_call(
        kernel,
        in_specs=[pl.BlockSpec(memory_space=VMEM) for _ in range(inputs)],
        out_specs=out_specs[0] if single else out_specs,
        out_shape=shapes[0] if single else shapes,
        scratch_shapes=list(scratch),
        compiler_params=pltpu.CompilerParams(vmem_limit_bytes=VMEM_LIMIT),
        name=kernel.__name__,
    )


WORDS = [SMEM((8, BLK), jnp.int32), pltpu.SemaphoreType.DMA]


def columns_of(blocks):
    return [VMEM((blocks * 4 + 8, BLK), f32), VMEM((blocks // 16, BLK, BLK), bf16)]


def accumulators(owners, number):
    return [VMEM(((owners + 1) * 8, BLK), f32) for _ in range(number)]


def on_device(source_cells, target_cells, start, source_logmass, target_logmass, pair_src, pair_tgt, pair_count):
    ring = [[z * 4 + r for z in range(16)] for r in range(4)]
    chips = [[z * 4 + r for r in range(4)] for z in range(16)]
    cores = [[i, i + 1] for i in range(0, 64, 2)]
    halves = [[2 * i + c for i in range(32)] for c in range(2)]
    to_chip = [(i, i ^ 2) for i in range(64)]

    source_mass = source_logmass.reshape(-1, BLK)
    target_mass = target_logmass.reshape(-1, BLK)

    mine = target_cells.T
    own = lax.all_to_all(jnp.broadcast_to(mine[None], (16, DIM, BLK)), "src", 0, 0, axis_index_groups=ring)
    other = lax.ppermute(own, "src", to_chip)
    own = lax.all_gather(own, "src", axis=0, axis_index_groups=cores)
    sources = source_cells.T
    table = ((8, BLK), jnp.int32)
    rows, norms, hot, info_s, info_t = call(
        prepare_kernel,
        4,
        [((128, BLK, BLK), bf16), ((128, BLK), f32), ((16, DIM, BLK), bf16), table, table],
    )(sources, pair_src.reshape(1, -1), pair_tgt.reshape(1, -1), pair_count)
    other, hot = lax.optimization_barrier((other, hot))
    other = lax.all_gather(other, "src", axis=0, axis_index_groups=cores)

    parts, target_rows, targets, start_v = call(
        first_kernel,
        7,
        [((8, 128, BLK), f32), ((64, BLK, BLK), bf16), ((64, DIM, BLK), bf16), ((64, BLK), f32)],
        WORDS + [VMEM((64, BLK), f32)] + columns_of(64) + accumulators(128, 3),
    )(info_s, sources, own, other, start.reshape(-1, BLK), norms, hot)
    parts = lax.all_to_all(parts, "tgt", 0, 0)
    lse, first_u = call(
        second_kernel,
        7,
        [((4, 16, BLK), f32), ((128, BLK), f32)],
        WORDS + columns_of(128) + accumulators(64, 3),
    )(info_t, rows, targets, parts, source_mass, start_v, hot)
    lse = lax.all_to_all(lse, "src", 0, 0, axis_index_groups=chips)
    lse = call(group_kernel, 1, [((16, 16, BLK), f32)])(lse)
    lse = lax.all_to_all(lse, "src", 0, 0, axis_index_groups=ring)
    lse = call(ring_kernel, 1, [((16, BLK), f32)])(lse)
    lse = lax.all_gather(lse, "src", axis=0, axis_index_groups=chips, tiled=True)
    parts, first_v, base = call(
        third_kernel,
        8,
        [((8, 128, BLK), f32), ((64, BLK), f32), ((1, BLK), f32)],
        WORDS + columns_of(64) + accumulators(128, 2),
    )(info_s, sources, target_rows, lse, target_mass, first_u, hot, mine)
    parts = lax.all_to_all(parts, "tgt", 0, 0)
    sums, last_u, odd = call(
        fourth_kernel,
        9,
        [((2, 32, BLK), f32), ((128, BLK), f32), ((32, BLK), jnp.int32)],
        WORDS + [VMEM((72, BLK), f32)] + columns_of(128) + accumulators(64, 2),
    )(info_t, rows, targets, parts, source_mass, first_u, first_v, norms, hot)
    sums = lax.all_gather(sums, "src", axis=0, axis_index_groups=cores)
    sums = call(total_kernel, 2, [((32, 1, BLK), f32)])(sums, odd)
    sums = lax.all_to_all(sums, "src", 0, 0, axis_index_groups=halves)
    last_v = call(last_kernel, 2, [((1, BLK), f32)])(sums, base)
    return last_u.reshape(-1), last_v.reshape(-1)


def solution(mesh):
    in_specs = (
        P("src", None),
        P(("tgt", "src"), None),
        P("tgt"),
        P("src"),
        P("tgt"),
        P("src", "tgt", None),
        P("src", "tgt", None),
        P("src", "tgt"),
    )
    out_specs = (P("src"), P(("tgt", "src")))
    return jax.shard_map(
        on_device, mesh=mesh, in_specs=in_specs, out_specs=out_specs, check_vma=False
    )
```

```python
import functools

import jax
import jax.numpy as jnp
from jax import lax
from jax.experimental import pallas as pl
from jax.experimental.pallas import tpu as pltpu
from jax.sharding import PartitionSpec as P

DIM = 64
BLK = 128
EPS = 0.1
SCALE = 2.0 / (DIM * EPS)
LOG2E = 1.4426950408889634
LN2 = 0.6931471805599453
KAPPA = SCALE * LOG2E
LOWEST = -1e30
LEAST, MOST = 2.0**-80, 2.0**120
LIFT = 100.0
OWNER = 20
VMEM_LIMIT = 16 * 1024 * 1024
STEP_BITS = 7
UNROLL = 1 << STEP_BITS
VMEM = pltpu.VMEM
SMEM = pltpu.SMEM
bf16 = jnp.bfloat16
f32 = jnp.float32


def block_of(n):
    return pl.ds(pl.multiple_of(n * BLK, BLK), BLK)


def as_rows(block):
    return jnp.concatenate([block, jnp.zeros((BLK - DIM, BLK), bf16)], axis=0).T


def norm_row(block):
    x = block.astype(f32)
    return jnp.sum(x * x, axis=0, keepdims=True)


def spread(potential, columns_ref, extra_ref):
    blocks = potential.shape[0]
    beta = potential * (1.0 / SCALE)
    hi = beta.astype(bf16).astype(f32)
    rest = beta - hi
    mid = rest.astype(bf16).astype(f32)
    for s, part in enumerate((hi, mid, rest - mid, jnp.zeros_like(hi))):
        columns_ref[pl.ds(s, blocks, stride=4), :] = part
    for g in range(blocks // 16):
        half = columns_ref[g * 64 : g * 64 + 64, :]
        extra_ref[g] = jnp.concatenate([jnp.zeros_like(half), half], axis=0).T.astype(bf16)


def pair_tile(x_ref, extra_ref, hot_ref, x_place, x_id, other_block):
    left = x_ref[x_place] + extra_ref[x_id >> 4]
    right = jnp.concatenate([other_block, hot_ref[x_id & 15]], axis=0)
    return jnp.dot(left, right, preferred_element_type=f32).reshape(16, 8, BLK)


def over_pairs(info, work, bits=STEP_BITS):
    def group(n, carry):
        row, first = 1 + (n >> (7 - bits)), (n << bits) & 127
        work([info[row, first + q] for q in range(1 << bits)])
        return carry

    lax.fori_loop(0, (info[0, 0] + ((1 << bits) - 1)) >> bits, group, 0)


def owner_rows(code):
    return pl.ds(pl.multiple_of(code >> OWNER, 8), 8)


def strided(acc, g):
    return [acc[pl.ds(g * 64 + s, 8, stride=8), :] for s in range(8)]


def stable_lse(info, tile, top, total, owners):
    top[...] = jnp.full(top.shape, LOWEST, f32)
    total[...] = jnp.zeros(total.shape, f32)

    def work(slots):
        stats = []
        for s in slots:
            z = tile(s)
            most = jnp.max(z, axis=0)
            stats.append((most, jnp.sum(jnp.exp2((z - most[None]) * KAPPA), axis=0)))
        for s, (most, part) in zip(slots, stats):
            rows = owner_rows(s)
            old = top[rows, :]
            new = jnp.maximum(old, most)
            total[rows, :] = total[rows, :] * jnp.exp2((old - new) * KAPPA) + part * jnp.exp2((most - new) * KAPPA)
            top[rows, :] = new

    over_pairs(info, work, 3)
    out = []
    for g in range(owners // 8):
        rows = strided(top, g)
        most = functools.reduce(jnp.maximum, rows)
        parts = [p * jnp.exp2((r - most) * KAPPA) for r, p in zip(rows, strided(total, g))]
        whole = functools.reduce(jnp.add, parts)
        out.append(jnp.where(whole > 0.0, most * SCALE + jnp.log(jnp.maximum(whole, 1e-30)), LOWEST))
    return jnp.concatenate(out, axis=0)


def plain_sum(info, tile, total, owners, offset, seen=None):
    total[...] = jnp.zeros(total.shape, f32)
    if seen is not None:
        seen[...] = jnp.zeros(seen.shape, f32)

    def work(slots):
        parts = []
        for s in slots:
            parts.append(jnp.sum(jnp.exp2(tile(s) * KAPPA + offset[owner_rows(s), :][None]), axis=0))
        for s, part in zip(slots, parts):
            rows = owner_rows(s)
            total[rows, :] = total[rows, :] + part
            if seen is not None:
                seen[rows, :] = jnp.ones((8, BLK), f32)

    over_pairs(info, work)
    return jnp.concatenate([functools.reduce(jnp.add, strided(total, g)) for g in range(owners // 8)], axis=0)


def guarded_lse(info, tile, accs, owners, values, offset, write):
    total_ref, seen_ref = accs
    repeat_rows(values, offset)
    total = plain_sum(info, tile, total_ref, owners, offset, seen_ref)
    seen = seen_ref[pl.ds(0, owners, stride=8), :] > 0.0
    fine = (total >= LEAST) & (total <= MOST)
    write(jnp.where(seen, jnp.log(jnp.where(fine, total, 1.0)) - values * LN2, LOWEST))
    lost = jnp.max(jnp.where(seen & jnp.logical_not(fine), 1.0, 0.0))

    @pl.when(lost > 0.0)
    def again():
        write(stable_lse(info, tile, total_ref, seen_ref, owners))


def repeat_rows(values, offset):
    owners = values.shape[0]
    for k in range(8):
        offset[pl.ds(k, owners, stride=8), :] = values
    offset[pl.ds(owners * 8, 8), :] = jnp.zeros((8, BLK), f32)


def by_source(targets, sources, extra, hot):
    def tile(code):
        at = pl.multiple_of(code & 0x3F80, BLK)
        return pair_tile(targets, extra, hot, (code >> 14) & 63, code & 63, sources[:, pl.ds(at, BLK)])

    return tile


def by_target(sources, targets, extra, hot):
    def tile(code):
        s = code & 127
        return pair_tile(sources, extra, hot, s, s, targets[(code >> 14) & 63])

    return tile


def prepare_kernel(sources, pair_src, pair_tgt, pair_count, rows, norms, hot, by_src, by_tgt):
    me = lax.axis_index("src")
    lane = lax.broadcasted_iota(jnp.int32, (1, BLK), 1)
    count = jnp.broadcast_to(pair_count[...], (1, BLK))
    by_src[0:1, :] = count
    by_tgt[0:1, :] = count
    for half in range(2):
        used = lane + half * BLK < count
        part = slice(half * BLK, (half + 1) * BLK)
        s, t = jnp.where(used, pair_src[:, part], 0), jnp.where(used, pair_tgt[:, part], 0)
        place = (((t ^ (me & 2)) & 3) << 4) + (t >> 2)
        by_src[half + 1 : half + 2, :] = t + (s << 7) + (place << 14) + (jnp.where(used, s, 128) << (OWNER + 3))
        by_tgt[half + 1 : half + 2, :] = s + (place << 14) + (jnp.where(used, t, 64) << (OWNER + 3))
    line = lax.broadcasted_iota(jnp.int32, (DIM, BLK), 0)
    for r in range(16):
        hot[r] = jnp.where((line >= 4 * r) & (line < 4 * r + 3), 1.0, 0.0).astype(bf16)
    for b in range(128):
        block = sources[:, b * BLK : b * BLK + BLK]
        rows[b] = as_rows(block)
        norms[b : b + 1, :] = norm_row(block)


def merge_lse(parts_ref):
    top = jnp.max(parts_ref[...], axis=0)
    total = jnp.sum(jnp.exp(parts_ref[...] - top[None]), axis=0)
    return top + jnp.log(total)


def ring_place(k, core):
    return (k + 8 * core) % 16


def first_kernel(
    words, sources, own, other, start, source_norms, hot,
    out, rows, targets, potential, info, arrival, norms, columns, extra, offset, *accs,
):
    coming = pltpu.make_async_copy(words, info, arrival)
    coming.start()
    mine = lax.axis_index("src") & 2
    for d in range(4):
        for k in range(16):
            z = ring_place(k, d & 1)
            block = (own, other)[d >> 1][d & 1, k]
            targets[d * 16 + z] = block
            rows[d * 16 + z] = as_rows(block)
            norms[pl.ds(z * 4 + (d ^ mine), 1), :] = norm_row(block)
    new = start[...] * (1.0 / EPS) - norms[...] * (SCALE / 2)
    potential[...] = new
    spread(new, columns, extra)
    coming.wait()
    tile = by_source(rows, sources, extra, hot)

    def write(lse):
        for k in range(8):
            out[k] = lse

    guarded_lse(info, tile, accs, 128, source_norms[...] * (-LOG2E * SCALE / 2), offset, write)


def second_kernel(
    words, rows, targets, parts, mass, former, hot, out, potential, info, arrival, columns, extra, offset, *accs
):
    coming = pltpu.make_async_copy(words, info, arrival)
    coming.start()
    new = mass[...] - merge_lse(parts)
    potential[...] = new
    spread(new, columns, extra)
    coming.wait()
    tile = by_target(rows, targets, extra, hot)

    def write(lse):
        for k in range(4):
            out[k] = lse[16 * k : 16 * k + 16]

    guarded_lse(info, tile, accs, 64, former[...] * LOG2E + LIFT, offset, write)


def group_kernel(parts, out):
    lse = merge_lse(parts)
    for k in range(16):
        out[k] = lse


def ring_kernel(parts, out):
    out[...] = merge_lse(parts)


def third_kernel(
    words, sources, rows, lse, mass, reference, hot, mine,
    out, potential, base, info, arrival, columns, extra, offset, acc,
):
    coming = pltpu.make_async_copy(words, info, arrival)
    coming.start()
    me = lax.axis_index("src")
    new = mass[...] - lse[...]
    potential[...] = new
    base[...] = potential[pl.ds(me, 1), :] + mass[pl.ds(me, 1), :] + norm_row(mine[...]) * (SCALE / 2)
    spread(new, columns, extra)
    repeat_rows(reference[...] * LOG2E, offset)
    coming.wait()
    tile = by_source(rows, sources, extra, hot)
    total = plain_sum(info, tile, acc, 128, offset)
    for k in range(8):
        out[k] = total


def fourth_kernel(
    words, rows, targets, parts, mass, former, reference, norms, hot,
    out, final, odd, info, arrival, held, columns, extra, offset, acc,
):
    coming = pltpu.make_async_copy(words, info, arrival)
    coming.start()
    new = former[...] + mass[...] - jnp.log(jnp.sum(parts[...], axis=0))
    spread(new, columns, extra)
    final[...] = EPS * (new + norms[...] * (SCALE / 2))
    odd[...] = jnp.full(odd.shape, lax.axis_index("src") & 1, jnp.int32)
    repeat_rows(reference[...] * LOG2E, offset)
    coming.wait()
    tile = by_target(rows, targets, extra, hot)
    held[pl.ds(0, 64), :] = plain_sum(info, tile, acc, 64, offset)
    for k in range(2):
        out[k] = held[pl.ds(k, 32, stride=2), :]


def total_kernel(parts, odd, out):
    second = parts[0, 1] + parts[1, 1]
    second = jnp.concatenate([second[16:], second[:16]], axis=0)
    out[...] = jnp.where(odd[...] == 0, parts[0, 0] + parts[1, 0], second)[:, None, :]


def last_kernel(parts, base, out):
    out[...] = EPS * (base[...] - jnp.log(jnp.sum(parts[...], axis=0)))


def call(kernel, inputs, outs, scratch=()):
    out_specs = [pl.BlockSpec(memory_space=VMEM) for _ in outs]
    shapes = [jax.ShapeDtypeStruct(shape, dtype) for shape, dtype in outs]
    single = len(outs) == 1
    return pl.pallas_call(
        kernel,
        in_specs=[pl.BlockSpec(memory_space=VMEM) for _ in range(inputs)],
        out_specs=out_specs[0] if single else out_specs,
        out_shape=shapes[0] if single else shapes,
        scratch_shapes=list(scratch),
        compiler_params=pltpu.CompilerParams(vmem_limit_bytes=VMEM_LIMIT),
        name=kernel.__name__,
    )


WORDS = [SMEM((8, BLK), jnp.int32), pltpu.SemaphoreType.DMA]


def columns_of(blocks):
    return [VMEM((blocks * 4 + 8, BLK), f32), VMEM((blocks // 16, BLK, BLK), bf16)]


def accumulators(owners, number):
    return [VMEM(((owners + 1) * 8, BLK), f32) for _ in range(number)]


def on_device(source_cells, target_cells, start, source_logmass, target_logmass, pair_src, pair_tgt, pair_count):
    ring = [[ring_place(k, r & 1) * 4 + r for k in range(16)] for r in range(4)]
    chips = [[z * 4 + r for r in range(4)] for z in range(16)]
    cores = [[i, i + 1] for i in range(0, 64, 2)]
    halves = [[2 * ((i + 16 * c) % 32) + c for i in range(32)] for c in range(2)]
    columns = [[8 * i + (k + 4 * (i & 1)) % 8 for k in range(8)] for i in range(64)]
    to_chip = [(i, i ^ 2) for i in range(64)]

    source_mass = source_logmass.reshape(-1, BLK)
    target_mass = target_logmass.reshape(-1, BLK)

    mine = target_cells.T
    own = lax.all_to_all(jnp.broadcast_to(mine[None], (16, DIM, BLK)), "src", 0, 0, axis_index_groups=ring)
    other = lax.ppermute(own, "src", to_chip)
    own = lax.all_gather(own, "src", axis=0, axis_index_groups=cores)
    sources = source_cells.T
    table = ((8, BLK), jnp.int32)
    rows, norms, hot, info_s, info_t = call(
        prepare_kernel,
        4,
        [((128, BLK, BLK), bf16), ((128, BLK), f32), ((16, DIM, BLK), bf16), table, table],
    )(sources, pair_src.reshape(1, -1), pair_tgt.reshape(1, -1), pair_count)
    other, hot = lax.optimization_barrier((other, hot))
    other = lax.all_gather(other, "src", axis=0, axis_index_groups=cores)

    parts, target_rows, targets, start_v = call(
        first_kernel,
        7,
        [((8, 128, BLK), f32), ((64, BLK, BLK), bf16), ((64, DIM, BLK), bf16), ((64, BLK), f32)],
        WORDS + [VMEM((64, BLK), f32)] + columns_of(64) + accumulators(128, 3),
    )(info_s, sources, own, other, start.reshape(-1, BLK), norms, hot)
    parts = lax.all_to_all(parts, ("src", "tgt"), 0, 0, axis_index_groups=columns)
    lse, first_u = call(
        second_kernel,
        7,
        [((4, 16, BLK), f32), ((128, BLK), f32)],
        WORDS + columns_of(128) + accumulators(64, 3),
    )(info_t, rows, targets, parts, source_mass, start_v, hot)
    lse = lax.all_to_all(lse, "src", 0, 0, axis_index_groups=chips)
    lse = call(group_kernel, 1, [((16, 16, BLK), f32)])(lse)
    lse = lax.all_to_all(lse, "src", 0, 0, axis_index_groups=ring)
    lse = call(ring_kernel, 1, [((16, BLK), f32)])(lse)
    lse = lax.all_gather(lse, "src", axis=0, axis_index_groups=chips, tiled=True)
    parts, first_v, base = call(
        third_kernel,
        8,
        [((8, 128, BLK), f32), ((64, BLK), f32), ((1, BLK), f32)],
        WORDS + columns_of(64) + accumulators(128, 2),
    )(info_s, sources, target_rows, lse, target_mass, first_u, hot, mine)
    parts = lax.all_to_all(parts, ("src", "tgt"), 0, 0, axis_index_groups=columns)
    sums, last_u, odd = call(
        fourth_kernel,
        9,
        [((2, 32, BLK), f32), ((128, BLK), f32), ((32, BLK), jnp.int32)],
        WORDS + [VMEM((72, BLK), f32)] + columns_of(128) + accumulators(64, 2),
    )(info_t, rows, targets, parts, source_mass, first_u, first_v, norms, hot)
    sums = lax.all_gather(sums, "src", axis=0, axis_index_groups=cores)
    sums = call(total_kernel, 2, [((32, 1, BLK), f32)])(sums, odd)
    sums = lax.all_to_all(sums, "src", 0, 0, axis_index_groups=halves)
    last_v = call(last_kernel, 2, [((1, BLK), f32)])(sums, base)
    return last_u.reshape(-1), last_v.reshape(-1)


def solution(mesh):
    in_specs = (
        P("src", None),
        P(("tgt", "src"), None),
        P("tgt"),
        P("src"),
        P("tgt"),
        P("src", "tgt", None),
        P("src", "tgt", None),
        P("src", "tgt"),
    )
    out_specs = (P("src"), P(("tgt", "src")))
    return jax.shard_map(
        on_device, mesh=mesh, in_specs=in_specs, out_specs=out_specs, check_vma=False
    )
```
